256 devices in a mesh: section: 32 (over z, x_lo, core), tp: 8 (over y, x_hi).
Axes of the slice: x: 4 (x_hi: 2, x_lo: 2; x = x_hi * 2 + x_lo), y: 4, z: 8, core: 2. Of those that a mesh axis runs over, the one named last changes fastest.
Arguments:
- layer_outputs: bfloat16 [32, 128, 8192], P('section', None, 'tp'), may hold values from -72 to 72
- stream_grads: bfloat16 [32, 3, 128, 8192], P('section', None, None, 'tp'), may hold values from -0.3125 to 0.3125
- residual_grads: bfloat16 [32, 128, 8192], P('section', None, 'tp'), may hold values from -0.4375 to 0.4375
- norm_gain: bfloat16 [32, 8192], P('section', 'tp'), may hold values from 0.5 to 1.5
- first_weight: bfloat16 [32, 8192, 384], P('section', 'tp'), may hold values from -0.0625 to 0.0625
- second_weight: bfloat16 [32, 384, 96], P('section'), may hold values from -0.3125 to 0.3125
Outputs:
- stream_grad: bfloat16 [32, 128, 8192], P('section', None, 'tp')
- first_grad: float32 [32, 8192, 384], P('section', 'tp')
- second_grad: float32 [32, 384, 96], P('section')
The draws below stay inside these ranges and needn't reach their ends.
All inputs are finite; a program needn't handle non-finite values.
Results may differ from the reference program's by a relative error of at most 0.008.
Values may be sent and summed in bfloat16 or wider, within the bound.
A program may use at most 128 MiB of HBM per device.

```python
import jax
import jax.numpy as jnp
from jax import lax

D = 8192
KH = 384
TOK_DEV = 128
LAYERS = 32


def draw_layer_outputs(key, part):
    key = jax.random.fold_in(key, 7)
    key_base, key_row, key_col = jax.random.split(key, 3)
    base = jnp.clip(jax.random.normal(key_base, (LAYERS, TOK_DEV, D), jnp.float32), -4.0, 4.0)
    row_scale = jnp.exp(jax.random.uniform(key_row, (LAYERS, TOK_DEV, 1), jnp.float32, -1.15, 1.15))
    rising = 3.0 ** (jnp.arange(D, dtype=jnp.float32) / D)
    col_scale = jnp.exp(jax.random.uniform(key_col, (1, 1, D), jnp.float32, -1.15, 1.15)) * rising / 1.7
    return (base * row_scale * col_scale).astype(jnp.bfloat16)


def block_levels(key, extent, cuts, least, largest):
    factor_of, own = 1.0, jax.random.fold_in(key, 6)
    for position, parts in cuts:
        steps = jnp.exp(jax.random.uniform(jax.random.fold_in(own, position), (parts,), jnp.float32, least / len(cuts), largest / len(cuts)))
        factor_of = factor_of * jnp.repeat(steps, extent[position] // parts).reshape([-1 if axis == position else 1 for axis in range(len(extent))])
    return factor_of


def scatter_about(stream_key, extent, width, bound, cuts=(), held_as=jnp.bfloat16):
    loudness = block_levels(stream_key, extent, cuts, -0.22, 0.18) if cuts else 1.0
    values = jax.random.normal(stream_key, extent, jnp.float32) * width * loudness
    return jnp.minimum(jnp.maximum(values, -bound), bound).astype(held_as)


def setup_inputs(seed: int = 0) -> dict:
    key_of = jax.random.split(jax.random.key(seed), 7)
    return {
        "layer_outputs": draw_layer_outputs(jax.random.fold_in(key_of[6], 71), 0),
        "stream_grads": scatter_about(key_of[1], (LAYERS, 3, TOK_DEV, D), 0.02, 0.3125, ((0, 32), (3, 8))),
        "residual_grads": scatter_about(key_of[2], (LAYERS, TOK_DEV, D), 0.03, 0.4375, ((0, 32), (2, 8))),
        "norm_gain": jnp.clip(1.0 + 0.1 * jax.random.normal(key_of[3], (LAYERS, D), jnp.float32), 0.5, 1.5).astype(jnp.bfloat16),
        "first_weight": scatter_about(key_of[4], (LAYERS, D, KH), D ** -0.5, 0.0625, ((0, 32), (1, 8))),
        "second_weight": scatter_about(key_of[5], (LAYERS, KH, 3 * LAYERS), KH ** -0.5, 0.3125, ((0, 32),)),
    }


def gelu_grad(pre_act, upstream):
    value, pullback = jax.vjp(jax.nn.gelu, pre_act)
    return pullback(upstream)[0]

def reference(layer_outputs, stream_grads, residual_grads, norm_gain, first_weight, second_weight):
    outputs_all = layer_outputs.astype(jnp.float32)
    depth_ids = jnp.arange(LAYERS, dtype=jnp.int32)

    def one_layer(totals, index):
        inputs = outputs_all[index]
        inverse = lax.rsqrt(lax.optimization_barrier(jnp.mean(inputs * inputs, axis=1)) + 1e-05)[:, None]
        gain_row = norm_gain[index].astype(jnp.float32)
        normed = (inputs * inverse * gain_row).astype(jnp.bfloat16)
        pre_act = jnp.dot(normed, first_weight[index], preferred_element_type=jnp.float32)
        hidden = jax.nn.gelu(pre_act)
        second = second_weight[index].astype(jnp.float32)
        depth_mask = depth_ids <= index
        mixing = jnp.dot(hidden, second, precision=lax.Precision.HIGHEST).reshape(TOK_DEV, 3, LAYERS)
        mixing = jnp.where(depth_mask[None, None, :], mixing, 0.0)
        mixing_low = mixing.astype(jnp.bfloat16)
        streams = stream_grads[index].astype(jnp.float32)
        mix_grad = jnp.einsum('std,jtd->tsj', streams, outputs_all)
        mix_grad = jnp.where(depth_mask[None, None, :], mix_grad, 0.0)
        flat_grad = mix_grad.reshape(TOK_DEV, 3 * LAYERS)
        second_grad = jnp.dot(hidden.T, flat_grad, precision=lax.Precision.HIGHEST)
        hidden_grad = jnp.dot(flat_grad, second.T, precision=lax.Precision.HIGHEST)
        pre_grad = gelu_grad(pre_act, hidden_grad).astype(jnp.bfloat16)
        first_grad = jnp.dot(normed.T, pre_grad, preferred_element_type=jnp.float32)
        normed_grad = jnp.dot(pre_grad, first_weight[index].T, preferred_element_type=jnp.float32)
        scaled = normed_grad * gain_row
        along = lax.optimization_barrier(jnp.sum(scaled * inputs, axis=1))[:, None]
        local_grad = inverse * scaled - inputs * inverse ** 3 * along / D
        partial_value = jnp.einsum('tsj,std->jtd', mixing_low.astype(jnp.float32), streams)
        return (totals + partial_value, (local_grad, first_grad, second_grad))
    start = jnp.zeros((LAYERS, TOK_DEV, D), jnp.float32)
    totals, (local_all, first_all, second_all) = lax.scan(one_layer, start, depth_ids)
    residual = residual_grads.astype(jnp.float32)
    carried = jnp.cumsum(residual[::-1], axis=0)[::-1]
    stream_grad = (totals + carried + local_all).astype(jnp.bfloat16)
    return (stream_grad, first_all, second_all)
```

```python
import functools

import jax
import jax.numpy as jnp
from jax import lax
from jax.experimental import pallas as pl
from jax.experimental.pallas import tpu as pltpu
from jax.sharding import PartitionSpec as P

MESH = pl.DeviceIdType.MESH
F32, BF16 = jnp.float32, jnp.bfloat16
SECTIONS, SHARDS = 32, 8
TOKENS, WIDTH, HIDDEN = 128, 1024, 384
FULL_WIDTH = WIDTH * SHARDS
C0, C1 = 0.7978845608028654, 0.044715


def dot(a, b):
    return jnp.dot(a, b, preferred_element_type=F32)


def dot_nt(a, b):
    return lax.dot_general(a, b, (((1,), (1,)), ((), ())), preferred_element_type=F32)


def dot_tn(a, b):
    return lax.dot_general(a, b, (((0,), (0,)), ((), ())), preferred_element_type=F32)


def halves(v):
    high = v.astype(BF16)
    return high, (v - high.astype(F32)).astype(BF16)


def grid(rows, columns):
    return (
        lax.broadcasted_iota(jnp.int32, (rows, columns), 0),
        lax.broadcasted_iota(jnp.int32, (rows, columns), 1),
    )


def pick(condition):
    return jnp.where(condition, 1.0, 0.0).astype(BF16)


def kernel(
    x_hbm, g_hbm, r_hbm, gain_ref, w1_hbm, w2_ref,
    out_hbm, first_hbm, second_hbm,
    stage, r_stage, w1, sent, held, r_sent, r_held, w_sent, w_held, o_sent, o_held,
    z_sent, z_held, act, d_sent, d_held, e_sent, e_held,
    out_v, first_v, second_v, normed_t,
    in_sem, out_sem, x_ss, x_rs, r_ss, r_rs, w_ss, w_rs, o_ss, o_rs,
    z_ss, z_rs, a_ss, a_rs, d_ss, d_rs, e_ss, e_rs,
):
    me = lax.axis_index("section")
    part = lax.axis_index("tp")

    loads = []
    for b in range(2):
        rows = pl.ds(64 * b, 64)
        for s in range(3):
            loads.append(pltpu.make_async_copy(g_hbm.at[0, s, rows], stage.at[b, s], in_sem.at[len(loads)]))
        loads.append(pltpu.make_async_copy(x_hbm.at[0, rows], stage.at[b, 3], in_sem.at[len(loads)]))
    loads.append(pltpu.make_async_copy(w1_hbm.at[0], w1, in_sem.at[len(loads)]))
    for b in range(2):
        for f in range(4):
            loads.append(
                pltpu.make_async_copy(
                    r_hbm.at[0, pl.ds(64 * b, 64), pl.ds(256 * f, 256)], r_stage.at[b, f], in_sem.at[len(loads)]
                )
            )
    for load in loads:
        load.start()

    barrier = pltpu.get_barrier_semaphore()

    def greet_section(n, c):
        pl.semaphore_signal(barrier, inc=1, device_id={"section": lax.rem(me + n, SECTIONS)}, device_id_type=MESH)
        return c

    def greet_part(n, c):
        pl.semaphore_signal(barrier, inc=1, device_id={"tp": lax.rem(part + n, SHARDS)}, device_id_type=MESH)
        return c

    lax.fori_loop(1, SECTIONS, greet_section, 0)
    lax.fori_loop(1, SHARDS, greet_part, 0)

    def section_copy(src, dst, ss, rs, to, slot):
        return pltpu.make_async_remote_copy(
            src_ref=src.at[to], dst_ref=dst.at[slot], send_sem=ss.at[to], recv_sem=rs.at[slot],
            device_id={"section": to}, device_id_type=MESH,
        )

    def part_copy(src, dst, ss, rs, to, slot):
        return pltpu.make_async_remote_copy(
            src_ref=src, dst_ref=dst.at[slot], send_sem=ss.at[to], recv_sem=rs.at[slot],
            device_id={"tp": to}, device_id_type=MESH,
        )

    def send_sections(src, dst, ss, rs):
        def step(n, c):
            section_copy(src, dst, ss, rs, lax.rem(me + n, SECTIONS), me).start()
            return c

        lax.fori_loop(1, SECTIONS, step, 0)

    def await_sections(src, dst, ss, rs):
        def step(n, c):
            peer = lax.rem(me + n, SECTIONS)
            section_copy(src, dst, ss, rs, peer, peer).wait_recv()
            return c

        lax.fori_loop(1, SECTIONS, step, 0)

    def drain_sections(src, dst, ss, rs):
        def step(n, c):
            section_copy(src, dst, ss, rs, lax.rem(me + n, SECTIONS), me).wait_send()
            return c

        lax.fori_loop(1, SECTIONS, step, 0)

    def send_parts(pick_src, dst, ss, rs):
        def step(n, c):
            peer = lax.rem(part + n, SHARDS)
            part_copy(pick_src(peer), dst, ss, rs, peer, part).start()
            return c

        lax.fori_loop(1, SHARDS, step, 0)

    def await_parts(pick_src, dst, ss, rs):
        def step(n, c):
            peer = lax.rem(part + n, SHARDS)
            part_copy(pick_src(peer), dst, ss, rs, peer, peer).wait_recv()
            return c

        lax.fori_loop(1, SHARDS, step, 0)

    def drain_parts(pick_src, dst, ss, rs):
        def step(n, c):
            peer = lax.rem(part + n, SHARDS)
            part_copy(pick_src(peer), dst, ss, rs, peer, part).wait_send()
            return c

        lax.fori_loop(1, SHARDS, step, 0)

    row, col = grid(256, 256)
    regroup = pick(((row >> 2) & 3) * 64 + (row >> 4) * 4 + (row & 3) == col)

    gain = gain_ref[...].astype(F32)

    for b in range(2):
        for load in loads[4 * b : 4 * b + 4]:
            load.wait()
        grouped = dot(regroup, stage[b].reshape(256, WIDTH)).astype(BF16)
        sent[pl.ds(16 * b, 16)] = grouped.reshape(16, 16, WIDTH)

    loads[8].wait()
    for b in range(2):
        x = stage[b, 3].astype(F32)
        high, low = halves(x * gain)
        product = dot(high, w1[...]) + dot(low, w1[...])
        squares = jnp.sum(x * x, axis=1, keepdims=True)
        block = jnp.concatenate([product, jnp.broadcast_to(squares, (64, 128))], axis=1)
        z_sent[pl.ds(4 * b, 4)] = block.reshape(4, 16, 512)

    pl.semaphore_wait(barrier, SECTIONS - 1 + SHARDS - 1)

    z_src = lambda peer: z_sent.at[peer]
    send_parts(z_src, z_held, z_ss, z_rs)
    send_sections(sent, held, x_ss, x_rs)
    held[pl.ds(me, 1)] = sent[pl.ds(me, 1)]
    z_held[pl.ds(part, 1)] = z_sent[pl.ds(part, 1)]

    for load in loads[9:]:
        load.wait()
    for b in range(2):
        grouped = dot(regroup, r_stage[b].reshape(256, 256)).astype(BF16)
        r_sent[pl.ds(16 * b, 16)] = grouped.reshape(16, 16, 256)
    r_held[pl.ds(me, 1)] = r_sent[pl.ds(me, 1)]

    await_parts(z_src, z_held, z_ss, z_rs)
    total = z_held[0]
    for p in range(1, SHARDS):
        total = total + z_held[p]
    scale = lax.rsqrt(total[:, HIDDEN:] / FULL_WIDTH + 1e-05)
    own = jnp.concatenate([total[:, :HIDDEN] * scale[:, :1], scale], axis=1)
    act[pl.ds(part, 1)] = own.reshape(1, 16, 512)
    a_src = lambda peer: act.at[part]
    send_parts(a_src, act, a_ss, a_rs)
    send_sections(r_sent, r_held, r_ss, r_rs)
    row, col = grid(96, HIDDEN)
    w2 = w2_ref[0]
    w2_wide = dot(w2, pick(row == col >> 2)).astype(BF16)
    row, col = grid(96, 128)
    w2_pad = dot(w2, pick(row == col)).astype(BF16)
    await_parts(a_src, act, a_ss, a_rs)

    pre = act[:, :, :HIDDEN].reshape(TOKENS, HIDDEN)
    inverse = act[:, :, HIDDEN:].reshape(TOKENS, 128)[:, :1]
    square = pre * pre
    bend = jnp.tanh(C0 * pre * (1.0 + C1 * square))
    hidden = 0.5 * pre * (1.0 + bend)
    slope = 0.5 * (1.0 + bend) + 0.5 * pre * (1.0 - bend * bend) * (C0 * (1.0 + 3.0 * C1 * square))
    h_high, h_low = halves(hidden)
    mixing = dot(h_high, w2_wide) + dot(h_low, w2_wide)
    row, col = grid(TOKENS, HIDDEN)
    keep = ((row & 3) == (col & 3)) & (((col >> 2) & 31) <= me)
    mixing = jnp.where(keep, mixing, 0.0).astype(BF16)
    for b in range(2):
        block = mixing[64 * b : 64 * b + 64]
        stacked = jnp.concatenate(
            [block[:, :128], block[:, 128:256], block[:, 256:], jnp.zeros((64, 128), BF16)], axis=0
        )
        w_sent[pl.ds(16 * b, 16)] = dot(regroup, stacked).astype(BF16).reshape(16, 16, 128)
    w_held[pl.ds(me, 1)] = w_sent[pl.ds(me, 1)]
    send_sections(w_sent, w_held, w_ss, w_rs)

    for b in range(2):
        x = stage[b, 3].astype(F32)
        normed = (x * inverse[64 * b : 64 * b + 64] * gain).astype(BF16)
        normed_t[:, pl.ds(64 * b, 64)] = normed.T

    await_sections(sent, held, x_ss, x_rs)
    table = held[...].reshape(512, WIDTH)
    row, col = grid(128, 512)
    streams = dot(pick((row >> 2) * 16 + 12 + (row & 3) == col), table).astype(BF16)
    gram = dot_nt(table, streams)
    row, col = grid(512, 128)
    gram = jnp.where((row & 3) == (col & 3), gram, 0.0)
    rr, cc = grid(128, 128)
    spread = pick((rr >> 2) == (cc & 31))
    high, low = halves(gram)
    wide = dot(high, spread) + dot(low, spread)
    which = (row >> 2) & 3
    wide = jnp.where((which == (col >> 5)) & (which < 3) & ((col & 31) <= (row >> 4)), wide, 0.0)
    row, col = grid(128, 512)
    fold = pick(((row >> 2) == (col >> 4)) & ((row & 3) == (col & 3)))
    high, low = halves(wide)
    d_sent[...] = (dot(fold, high) + dot(fold, low)).reshape(SHARDS, 16, 128)
    d_src = lambda peer: d_sent.at[peer]
    send_parts(d_src, d_held, d_ss, d_rs)
    d_held[pl.ds(part, 1)] = d_sent[pl.ds(part, 1)]

    await_sections(w_sent, w_held, w_ss, w_rs)
    weights = w_held[...].reshape(512, 128).T
    partial = [dot(weights, table[:, 256 * f : 256 * f + 256]) for f in range(4)]
    await_sections(r_sent, r_held, r_ss, r_rs)
    row, col = grid(512, 512)
    later = pick(((row & 15) == (col & 15)) & ((col >> 4) >= (row >> 4)))
    carried = dot(later, r_held[...].reshape(512, 256))
    for b in range(2):
        stacked = jnp.concatenate([p[64 * b : 64 * b + 64] for p in partial], axis=0)
        high, low = halves(stacked)
        block = dot(regroup, high) + dot(regroup, low) + carried[256 * b : 256 * b + 256]
        o_sent[pl.ds(16 * b, 16)] = block.astype(BF16).reshape(16, 16, 256)
    o_held[pl.ds(me, 1)] = o_sent[pl.ds(me, 1)]

    await_parts(d_src, d_held, d_ss, d_rs)
    total = d_held[0]
    for p in range(1, SHARDS):
        total = total + d_held[p]
    for a in range(4):
        e_sent[a] = total[4 * a : 4 * a + 4]

    def e_copy(n):
        a, b = n // SHARDS, lax.rem(n, SHARDS)
        to = 4 * part + a
        return (to != me) | (b != part), pltpu.make_async_remote_copy(
            src_ref=e_sent.at[a], dst_ref=e_held.at[me], send_sem=e_ss.at[n], recv_sem=e_rs.at[me],
            device_id={"section": to, "tp": b}, device_id_type=MESH,
        )

    def e_send(n, c):
        away, copy = e_copy(n)

        @pl.when(away)
        def _():
            copy.start()

        return c

    def e_drain(n, c):
        away, copy = e_copy(n)

        @pl.when(away)
        def _():
            copy.wait_send()

        return c

    def e_await(n, c):
        @pl.when((n != me) | (me // 4 != part))
        def _():
            pltpu.make_async_remote_copy(
                src_ref=e_sent.at[0], dst_ref=e_held.at[n], send_sem=e_ss.at[0], recv_sem=e_rs.at[n],
                device_id={"section": n, "tp": me // 4}, device_id_type=MESH,
            ).wait_recv()

        return c

    lax.fori_loop(0, 32, e_send, 0)

    @pl.when(me // 4 == part)
    def _():
        e_held[pl.ds(me, 1)] = e_sent[pl.ds(lax.rem(me, 4), 1)]

    send_sections(o_sent, o_held, o_ss, o_rs)
    lax.fori_loop(0, SECTIONS, e_await, 0)

    mix_grad = e_held[...].reshape(TOKENS, 128)
    g_high, g_low = halves(mix_grad)
    pre_grad = ((dot_nt(g_high, w2_pad) + dot_nt(g_low, w2_pad)) * slope).astype(BF16)
    first_v[...] = dot(normed_t[...], pre_grad)
    first_out = pltpu.make_async_copy(first_v, first_hbm.at[0], out_sem.at[0])
    first_out.start()
    second = dot_tn(h_high, g_high) + dot_tn(h_high, g_low) + dot_tn(h_low, g_high)
    second_v[...] = second[:, :96]
    second_out = pltpu.make_async_copy(second_v, second_hbm.at[0], out_sem.at[1])
    second_out.start()
    along = jnp.sum(pre_grad.astype(F32) * pre, axis=1, keepdims=True)
    inner = inverse * inverse * along / FULL_WIDTH
    local = inverse * (dot_nt(pre_grad, w1[...]) * gain)

    await_sections(o_sent, o_held, o_ss, o_rs)
    for b in range(2):
        rows = slice(64 * b, 64 * b + 64)
        arrived = dot_tn(regroup, o_held[pl.ds(16 * b, 16)].reshape(256, 256))
        x = stage[b, 3].astype(F32)
        for f in range(4):
            lanes = slice(256 * f, 256 * f + 256)
            value = arrived[64 * f : 64 * f + 64] + (local[rows, lanes] - x[:, lanes] * inner[rows])
            out_v[pl.ds(64 * b, 64), pl.ds(256 * f, 256)] = value.astype(BF16)
    out_copy = pltpu.make_async_copy(out_v, out_hbm.at[0], out_sem.at[2])
    out_copy.start()

    drain_parts(z_src, z_held, z_ss, z_rs)
    drain_parts(a_src, act, a_ss, a_rs)
    drain_parts(d_src, d_held, d_ss, d_rs)
    drain_sections(sent, held, x_ss, x_rs)
    drain_sections(r_sent, r_held, r_ss, r_rs)
    drain_sections(w_sent, w_held, w_ss, w_rs)
    drain_sections(o_sent, o_held, o_ss, o_rs)
    lax.fori_loop(0, 32, e_drain, 0)
    first_out.wait()
    second_out.wait()
    out_copy.wait()


def local(layer_outputs, stream_grads, residual_grads, norm_gain, first_weight, second_weight):
    anywhere = pl.BlockSpec(memory_space=pl.ANY)
    vmem = pl.BlockSpec(memory_space=pltpu.VMEM)
    dma = pltpu.SemaphoreType.DMA
    by_section = lambda rows, lanes, dtype: pltpu.VMEM((SECTIONS, rows, lanes), dtype)
    by_part = lambda rows, lanes: pltpu.VMEM((SHARDS, rows, lanes), F32)
    return pl.pallas_call(
        kernel,
        out_shape=(
            jax.ShapeDtypeStruct((1, TOKENS, WIDTH), BF16),
            jax.ShapeDtypeStruct((1, WIDTH, HIDDEN), F32),
            jax.ShapeDtypeStruct((1, HIDDEN, 96), F32),
        ),
        in_specs=[anywhere, anywhere, anywhere, vmem, anywhere, vmem],
        out_specs=(anywhere, anywhere, anywhere),
        scratch_shapes=[
            pltpu.VMEM((2, 4, 64, WIDTH), BF16),
            pltpu.VMEM((2, 4, 64, 256), BF16),
            pltpu.VMEM((WIDTH, HIDDEN), BF16),
            by_section(16, WIDTH, BF16), by_section(16, WIDTH, BF16),
            by_section(16, 256, BF16), by_section(16, 256, BF16),
            by_section(16, 128, BF16), by_section(16, 128, BF16),
            by_section(16, 256, BF16), by_section(16, 256, BF16),
            by_part(16, 512), by_part(16, 512), by_part(16, 512),
            by_part(16, 128), by_part(16, 128),
            pltpu.VMEM((4, 4, 128), F32),
            by_section(4, 128, F32),
            pltpu.VMEM((TOKENS, WIDTH), BF16),
            pltpu.VMEM((WIDTH, HIDDEN), F32),
            pltpu.VMEM((HIDDEN, 96), F32),
            pltpu.VMEM((WIDTH, TOKENS), BF16),
            dma((17,)), dma((3,)),
            *[dma((SECTIONS,)) for _ in range(8)],
            *[dma((SHARDS,)) for _ in range(6)],
            dma((32,)), dma((32,)),
        ],
        compiler_params=pltpu.CompilerParams(
            collective_id=0, has_side_effects=True, vmem_limit_bytes=40 * 1024 * 1024
        ),
    )(layer_outputs, stream_grads, residual_grads, norm_gain, first_weight, second_weight)


def solution(mesh):
    placed = (
        P("section", None, "tp"),
        P("section", None, None, "tp"),
        P("section", None, "tp"),
        P("section", "tp"),
        P("section", "tp", None),
        P("section", None, None),
    )
    return jax.shard_map(
        local,
        mesh=mesh,
        in_specs=placed,
        out_specs=(P("section", None, "tp"), P("section", "tp", None), P("section", None, None)),
        check_vma=False,
    )
```

```python
import functools

import jax
import jax.numpy as jnp
from jax import lax
from jax.experimental import pallas as pl
from jax.experimental.pallas import tpu as pltpu
from jax.sharding import PartitionSpec as P

MESH = pl.DeviceIdType.MESH
F32, BF16 = jnp.float32, jnp.bfloat16
SECTIONS, SHARDS = 32, 8
PLANES, PLACES = 8, 4
TOKENS, WIDTH, HIDDEN = 128, 1024, 384
FULL_WIDTH = WIDTH * SHARDS
C0, C1 = 0.7978845608028654, 0.044715
FAR = [(4, q) for q in range(PLACES)]
MIDDLE = [(z, q) for q in range(PLACES) for z in (3, 5)]
CLOSE = [(z, q) for q in range(PLACES) for z in (2, 6)]
NEXT = [(z, q) for q in range(PLACES) for z in (1, 7)] + [(0, q) for q in range(1, PLACES)]
ALL = FAR + MIDDLE + CLOSE + NEXT


def dot(a, b):
    return jnp.dot(a, b, preferred_element_type=F32)


def dot_nt(a, b):
    return lax.dot_general(a, b, (((1,), (1,)), ((), ())), preferred_element_type=F32)


def dot_tn(a, b):
    return lax.dot_general(a, b, (((0,), (0,)), ((), ())), preferred_element_type=F32)


def halves(v):
    high = v.astype(BF16)
    return high, (v - high.astype(F32)).astype(BF16)


def grid(rows, columns):
    return (
        lax.broadcasted_iota(jnp.int32, (rows, columns), 0),
        lax.broadcasted_iota(jnp.int32, (rows, columns), 1),
    )


def pick(condition):
    return jnp.where(condition, 1.0, 0.0).astype(BF16)


def kernel(
    x_hbm, g_hbm, r_hbm, gain_hbm, w1_hbm, w2_hbm,
    out_v, first_v, second_v,
    stage, r_stage, gain_v, w1, w2, spread_m, sel_m, fold_m, normed_t,
    sent, held, r_sent, r_held, c_sent, c_held, s_sent, s_held, w_sent, w_held, o_sent, o_held,
    z_sent, z_held, act, d_sent, d_held, e_sent, e_held,
    in_sem, x_ss, x_rs, w_ss, w_rs, o_ss, o_rs, s_ss, s_rs,
    z_ss, z_rs, a_ss, a_rs, d_ss, d_rs, r_ss, r_rs, c_ss, c_rs, e_ss, e_rs,
):
    me = lax.axis_index("section")
    part = lax.axis_index("tp")
    plane, place = me >> 2, me & 3


    def section(offset):
        return ((plane + offset[0]) & 7) * PLACES + (place ^ offset[1])

    loads = []
    for b in range(2):
        rows = pl.ds(64 * b, 64)
        for s in range(3):
            loads.append((g_hbm.at[0, s, rows], stage.at[b, s]))
        loads.append((x_hbm.at[0, rows], stage.at[b, 3]))
    loads += [(gain_hbm, gain_v), (w1_hbm.at[0], w1)]
    for b in range(2):
        for f in range(4):
            loads.append((r_hbm.at[0, pl.ds(64 * b, 64), pl.ds(256 * f, 256)], r_stage.at[b, f]))
    loads.append((w2_hbm.at[0], w2.at[pl.ds(0, 96)]))
    loads = [pltpu.make_async_copy(src, dst, in_sem.at[n]) for n, (src, dst) in enumerate(loads)]
    for load in loads[:8]:
        load.start()

    barrier = pltpu.get_barrier_semaphore()

    def greet(device):
        pl.semaphore_signal(barrier, inc=1, device_id=device, device_id_type=MESH)

    for offset in ALL:
        greet({"section": section(offset)})
    for n in range(1, SHARDS):
        greet({"tp": part ^ n})
    for load in loads[8:]:
        load.start()

    class Exchange:
        def __init__(self, peers, here, device, block, landing, ss, rs):
            self.peers, self.here = peers, here

            def copy(to, slot):
                return pltpu.make_async_remote_copy(
                    src_ref=block(to), dst_ref=landing(slot), send_sem=ss.at[to], recv_sem=rs.at[slot],
                    device_id=device(to), device_id_type=MESH,
                )

            self.copy = copy

        def send(self, peers=None):
            for to in peers or self.peers:
                self.copy(to, self.here).start()

        def receive(self):
            for to in self.peers:
                self.copy(to, to).wait_recv()

        def drain(self):
            for to in self.peers:
                self.copy(to, self.here).wait_send()

    by_section = lambda to: {"section": to}
    by_part = lambda to: {"tp": to}
    by_place = lambda to: {"section": plane * PLACES + to}
    by_plane = lambda to: {"section": to * PLACES + place}
    far, middle, close, beside = ([section(offset) for offset in group] for group in (FAR, MIDDLE, CLOSE, NEXT))
    sections = far + middle + close + beside
    parts = [part ^ n for n in range(1, SHARDS)]
    places = [place ^ n for n in range(1, PLACES)]
    planes = [(plane + n) & 7 for n in (4, 3, 5, 2, 6, 1, 7)]
    xg = Exchange(sections, me, by_section, lambda p: sent.at[p], lambda p: held.at[p], x_ss, x_rs)
    wx = Exchange(sections, me, by_section, lambda p: w_sent.at[p], lambda p: w_held.at[p], w_ss, w_rs)
    ox = Exchange(sections, me, by_section, lambda p: o_sent.at[p], lambda p: o_held.at[p], o_ss, o_rs)
    zx = Exchange(parts, part, by_part, lambda p: z_sent.at[p], lambda p: z_held.at[p], z_ss, z_rs)
    ax = Exchange(parts, part, by_part, lambda p: act.at[part], lambda p: act.at[p], a_ss, a_rs)
    dx = Exchange(parts, part, by_part, lambda p: d_sent.at[p], lambda p: d_held.at[p], d_ss, d_rs)
    rx = Exchange(places, place, by_place, lambda p: r_sent.at[:, p], lambda p: r_held.at[p], r_ss, r_rs)
    cx = Exchange(places, place, by_place, lambda p: c_sent.at[p], lambda p: c_held.at[:, p], c_ss, c_rs)
    sx = Exchange(planes, plane, by_plane, lambda p: s_sent.at[p], lambda p: s_held.at[p], s_ss, s_rs)

    row, col = grid(256, 256)
    regroup = pick(((row >> 2) & 3) * 64 + (row >> 4) * 4 + (row & 3) == col)

    for b in range(2):
        for load in loads[4 * b : 4 * b + 4]:
            load.wait()
        grouped = dot(regroup, stage[b].reshape(256, WIDTH)).astype(BF16)
        sent[pl.ds(16 * b, 16)] = grouped.reshape(16, 16, WIDTH)
    pl.semaphore_wait(barrier, SECTIONS - 1 + SHARDS - 1)
    xg.send(far)
    held[pl.ds(me, 1)] = sent[pl.ds(me, 1)]

    loads[8].wait()
    loads[9].wait()
    gain = gain_v[...].astype(F32)
    x = jnp.concatenate([stage[0, 3], stage[1, 3]], axis=0).astype(F32)
    product = dot(jnp.concatenate(halves(x * gain), axis=0), w1[...])
    squares = jnp.broadcast_to(jnp.sum(x * x, axis=1, keepdims=True), (TOKENS, 128))
    z_sent[...] = jnp.concatenate([product[:TOKENS] + product[TOKENS:], squares], axis=1).reshape(SHARDS, 16, 512)
    zx.send()
    xg.send(middle)
    z_held[pl.ds(part, 1)] = z_sent[pl.ds(part, 1)]

    for load in loads[10:]:
        load.wait()
    for b in range(2):
        grouped = dot(regroup, r_stage[b].reshape(256, 256)).astype(BF16)
        r_sent[pl.ds(4 * b, 4)] = grouped.reshape(4, PLACES, 16, 256)
    rx.send()
    r_held[pl.ds(place, 1)] = r_sent[:, pl.ds(place, 1)].reshape(1, PLANES, 16, 256)

    zx.receive()
    total = z_held[0]
    for p in range(1, SHARDS):
        total = total + z_held[p]
    scale = lax.rsqrt(total[:, HIDDEN:] / FULL_WIDTH + 1e-05)
    own = jnp.concatenate([total[:, :HIDDEN] * scale[:, :1], scale], axis=1)
    act[pl.ds(part, 1)] = own.reshape(1, 16, 512)
    ax.send()
    xg.send(close)

    rx.receive()
    running = jnp.zeros((PLANES, 16, 256), F32)
    for p in reversed(range(PLACES)):
        running = running + r_held[p].astype(F32)
        c_sent[p] = running.astype(BF16)
    s_sent[...] = running.astype(BF16)
    c_held[:, pl.ds(place, 1)] = c_sent[pl.ds(place, 1)].reshape(PLANES, 1, 16, 256)
    s_held[pl.ds(plane, 1)] = s_sent[pl.ds(plane, 1)]
    cx.send()

    w2[pl.ds(96, 32)] = jnp.zeros((32, HIDDEN), BF16)
    ax.receive()
    pre = act[:, :, :HIDDEN].reshape(TOKENS, HIDDEN)
    inverse = act[:, :, HIDDEN:].reshape(TOKENS, 128)[:, :1]
    square = pre * pre
    bend = jnp.tanh(C0 * pre * (1.0 + C1 * square))
    hidden = 0.5 * pre * (1.0 + bend)
    slope = 0.5 * (1.0 + bend) + 0.5 * pre * (1.0 - bend * bend) * (C0 * (1.0 + 3.0 * C1 * square))
    h_high, h_low = halves(hidden)
    mixing = dot_nt(h_high, w2[...]) + dot_nt(h_low, w2[...])
    row, col = grid(TOKENS, 128)
    mixing = jnp.where((col & 31) <= me, mixing, 0.0)
    w_sent[...] = mixing.reshape(SECTIONS, 4, 128)
    w_held[pl.ds(me, 1)] = w_sent[pl.ds(me, 1)]
    wx.send()
    xg.send(beside)
    sx.send()

    row, col = grid(128, 512)
    sel_m[...] = pick((row >> 2) * 16 + 12 + (row & 3) == col)
    fold_m[...] = pick((((row >> 2) & 3) * SHARDS + (row >> 4) == (col >> 4)) & ((row & 3) == (col & 3)))
    row, col = grid(512, 128)
    spread_m[...] = pick(((row >> 4) == (col >> 2)) & ((row & 3) == (col & 3)))
    for b in range(2):
        x = stage[b, 3].astype(F32)
        normed = (x * inverse[64 * b : 64 * b + 64] * gain).astype(BF16)
        normed_t[:, pl.ds(64 * b, 64)] = normed.T

    xg.receive()
    table = held[...].reshape(512, WIDTH)
    streams = dot(sel_m[...], table).astype(BF16)
    gram = dot_nt(table, streams)
    row, col = grid(512, 128)
    gram = jnp.where((row & 3) == (col & 3), gram, 0.0)
    rr, cc = grid(128, 128)
    across = pick((rr >> 2) == (cc & 31))
    high, low = halves(gram)
    wide = dot(high, across) + dot(low, across)
    which = (row >> 2) & 3
    wide = jnp.where((which == (col >> 5)) & (which < 3) & ((col & 31) <= (row >> 4)), wide, 0.0)
    high, low = halves(wide)
    d_sent[...] = (dot(fold_m[...], high) + dot(fold_m[...], low)).reshape(SHARDS, 16, 128)
    dx.send()
    d_held[pl.ds(part, 1)] = d_sent[pl.ds(part, 1)]

    wx.receive()
    row, col = grid(128, 512)
    mixing = w_held[...].reshape(128, 128).astype(BF16)
    mixing = dot(mixing, pick(((row >> 5) == (col >> 7)) & ((row & 31) == ((col >> 2) & 31)))).astype(BF16)
    mixing = dot(spread_m[...], mixing)
    row, col = grid(512, 512)
    mixing = jnp.where((((row >> 2) & 3) == (col >> 7)) & ((row & 3) == (col & 3)), mixing, 0.0)
    weights = mixing[:, :128] + mixing[:, 128:256] + mixing[:, 256:384]
    weights = weights.astype(BF16).T
    partial = [dot(weights, table[:, 256 * f : 256 * f + 256]) for f in range(4)]
    sx.receive()
    running = jnp.zeros((16, 256), F32)
    carried = [None] * PLANES
    for p in reversed(range(PLANES)):
        carried[p] = jnp.concatenate([running] * PLACES, axis=0)
        running = running + s_held[p].astype(F32)
    for b in range(2):
        stacked = jnp.concatenate([p[64 * b : 64 * b + 64] for p in partial], axis=0)
        high, low = halves(stacked)
        block = dot(regroup, high) + dot(regroup, low) + jnp.concatenate(carried[4 * b : 4 * b + 4], axis=0)
        o_sent[pl.ds(16 * b, 16)] = block.astype(BF16).reshape(16, 16, 256)
    o_held[pl.ds(me, 1)] = o_sent[pl.ds(me, 1)]

    ox.send(far + middle)
    dx.receive()
    total = d_held[0]
    for p in range(1, SHARDS):
        total = total + d_held[p]
    for a in range(4):
        e_sent[a] = total[4 * a : 4 * a + 4]

    home, turn = me & 7, me >> 3

    def e_copy(a, b):
        return pltpu.make_async_remote_copy(
            src_ref=e_sent.at[a], dst_ref=e_held.at[me], send_sem=e_ss.at[a, b], recv_sem=e_rs.at[me],
            device_id={"section": SHARDS * a + part, "tp": b}, device_id_type=MESH,
        )

    def e_each(do):
        for n in range(1, SHARDS):
            for a in range(4):
                do(e_copy((turn + a) & 3, part ^ n))
        for a in range(4):

            @pl.when((home != part) | (turn != a))
            def _():
                do(e_copy(a, part))

    def e_receive(n):
        pltpu.make_async_remote_copy(
            src_ref=e_sent.at[0], dst_ref=e_held.at[n], send_sem=e_ss.at[0, 0], recv_sem=e_rs.at[n],
            device_id={"section": n, "tp": home}, device_id_type=MESH,
        ).wait_recv()

    e_each(lambda copy: copy.start())
    ox.send(close + beside)

    @pl.when(home == part)
    def _():
        e_held[pl.ds(me, 1)] = e_sent[pl.ds(turn, 1)]

    cx.receive()
    near = [dot_tn(regroup, c_held[pl.ds(4 * b, 4)].reshape(256, 256)) for b in range(2)]
    for exchange in (zx, ax, rx, cx, sx, xg, wx, dx):
        exchange.drain()

    for n in sections:
        e_receive(n)

    @pl.when(home != part)
    def _():
        e_receive(me)

    mix_grad = e_held[...].reshape(TOKENS, 128)
    g_high, g_low = halves(mix_grad)
    pre_grad = ((dot(g_high, w2[...]) + dot(g_low, w2[...])) * slope).astype(BF16)
    first_v[0] = dot(normed_t[...], pre_grad)
    second = dot_tn(g_high, h_high) + dot_tn(g_low, h_high) + dot_tn(g_high, h_low)
    second_v[0] = second[:96]
    along = jnp.sum(pre_grad.astype(F32) * pre, axis=1, keepdims=True)
    inner = inverse * inverse * along / FULL_WIDTH
    local = inverse * (dot_nt(pre_grad, w1[...]) * gain)

    ox.receive()
    for b in range(2):
        rows = slice(64 * b, 64 * b + 64)
        arrived = dot_tn(regroup, o_held[pl.ds(16 * b, 16)].reshape(256, 256)) + near[b]
        x = stage[b, 3].astype(F32)
        for f in range(4):
            lanes = slice(256 * f, 256 * f + 256)
            value = arrived[64 * f : 64 * f + 64] + (local[rows, lanes] - x[:, lanes] * inner[rows])
            out_v[0, pl.ds(64 * b, 64), pl.ds(256 * f, 256)] = value.astype(BF16)

    ox.drain()
    e_each(lambda copy: copy.wait_send())


def local(layer_outputs, stream_grads, residual_grads, norm_gain, first_weight, second_weight):
    hbm = pl.BlockSpec(memory_space=pltpu.HBM)
    vmem = pl.BlockSpec(memory_space=pltpu.VMEM)
    dma = pltpu.SemaphoreType.DMA
    by_section = lambda rows, lanes, dtype: pltpu.VMEM((SECTIONS, rows, lanes), dtype)
    by_part = lambda rows, lanes: pltpu.VMEM((SHARDS, rows, lanes), F32)
    by_place = lambda *lead: pltpu.VMEM((*lead, 16, 256), BF16)
    shapes = (
        jax.ShapeDtypeStruct((1, TOKENS, WIDTH), BF16),
        jax.ShapeDtypeStruct((1, WIDTH, HIDDEN), F32),
        jax.ShapeDtypeStruct((1, 96, HIDDEN), F32),
    )
    args = (layer_outputs, stream_grads, residual_grads, norm_gain, first_weight, jnp.swapaxes(second_weight, 1, 2))
    grads = pl.pallas_call(
        kernel,
        out_shape=shapes,
        in_specs=[hbm] * 6,
        out_specs=(vmem, vmem, vmem),
        scratch_shapes=[
            pltpu.VMEM((2, 4, 64, WIDTH), BF16),
            pltpu.VMEM((2, 4, 64, 256), BF16),
            pltpu.VMEM((1, WIDTH), BF16),
            pltpu.VMEM((WIDTH, HIDDEN), BF16),
            pltpu.VMEM((128, HIDDEN), BF16),
            pltpu.VMEM((512, 128), BF16),
            pltpu.VMEM((128, 512), BF16),
            pltpu.VMEM((128, 512), BF16),
            pltpu.VMEM((WIDTH, TOKENS), BF16),
            by_section(16, WIDTH, BF16), by_section(16, WIDTH, BF16),
            by_place(PLANES, PLACES), by_place(PLACES, PLANES),
            by_place(PLACES, PLANES), by_place(PLANES, PLACES),
            by_place(PLANES), by_place(PLANES),
            by_section(4, 128, F32), by_section(4, 128, F32),
            by_section(16, 256, BF16), by_section(16, 256, BF16),
            by_part(16, 512), by_part(16, 512), by_part(16, 512),
            by_part(16, 128), by_part(16, 128),
            pltpu.VMEM((4, 4, 128), F32),
            by_section(4, 128, F32),
            dma((19,)),
            *[dma((SECTIONS,)) for _ in range(6)],
            *[dma((PLANES,)) for _ in range(2)],
            *[dma((SHARDS,)) for _ in range(6)],
            *[dma((PLACES,)) for _ in range(4)],
            dma((4, SHARDS)), dma((SECTIONS,)),
        ],
        compiler_params=pltpu.CompilerParams(
            collective_id=0, has_side_effects=True, vmem_limit_bytes=32 * 1024 * 1024
        ),
    )(*[pltpu.with_memory_space_constraint(a, pltpu.HBM) for a in args])
    return grads[0], grads[1], jnp.swapaxes(grads[2], 1, 2)


def solution(mesh):
    placed = (
        P("section", None, "tp"),
        P("section", None, None, "tp"),
        P("section", None, "tp"),
        P("section", "tp"),
        P("section", "tp", None),
        P("section", None, None),
    )
    return jax.shard_map(
        local,
        mesh=mesh,
        in_specs=placed,
        out_specs=(P("section", None, "tp"), P("section", "tp", None), P("section", None, None)),
        check_vma=False,
    )
```

```python
import functools

import jax
import jax.numpy as jnp
from jax import lax
from jax.experimental import pallas as pl
from jax.experimental.pallas import tpu as pltpu
from jax.sharding import PartitionSpec as P

MESH = pl.DeviceIdType.MESH
F32, BF16 = jnp.float32, jnp.bfloat16
SECTIONS, SHARDS = 32, 8
PLANES, PLACES = 8, 4
TOKENS, WIDTH, HIDDEN = 128, 1024, 384
FULL_WIDTH = WIDTH * SHARDS
C0, C1 = 0.7978845608028654, 0.044715
FAR = [(4, q) for q in range(PLACES)]
MIDDLE = [(z, q) for q in range(PLACES) for z in (3, 5)]
CLOSE = [(z, q) for q in range(PLACES) for z in (2, 6)]
NEXT = [(z, q) for q in range(PLACES) for z in (1, 7)] + [(0, q) for q in range(1, PLACES)]
ALL = FAR + MIDDLE + CLOSE + NEXT
AROUND = (5, 7, 3, 4, 1, 6, 2)


def dot(a, b):
    return jnp.dot(a, b, preferred_element_type=F32)


def dot_nt(a, b):
    return lax.dot_general(a, b, (((1,), (1,)), ((), ())), preferred_element_type=F32)


def dot_tn(a, b):
    return lax.dot_general(a, b, (((0,), (0,)), ((), ())), preferred_element_type=F32)


def halves(v):
    high = v.astype(BF16)
    return high, (v - high.astype(F32)).astype(BF16)


def grid(rows, columns):
    return (
        lax.broadcasted_iota(jnp.int32, (rows, columns), 0),
        lax.broadcasted_iota(jnp.int32, (rows, columns), 1),
    )


def pick(condition):
    return jnp.where(condition, 1.0, 0.0).astype(BF16)


def kernel(
    x_hbm, g_hbm, r_hbm, gain_hbm, w1_hbm, w2_hbm,
    out_v, first_v, second_v,
    stage, r_stage, gain_v, w1, w2, spread_m, sel_m, fold_m, across_m, wide_m, same_m, kept_m, ungroup_m, normed_t,
    sent, held, r_sent, r_held, c_sent, c_held, s_sent, s_held, w_sent, w_held, o_sent, o_held,
    z_sent, z_held, act, d_sent, d_held, e_sent, e_held,
    in_sem, x_ss, x_rs, w_ss, w_rs, o_ss, o_rs, s_ss, s_rs,
    z_ss, z_rs, a_ss, a_rs, d_ss, d_rs, r_ss, r_rs, c_ss, c_rs, e_ss, e_rs,
):
    me = lax.axis_index("section")
    part = lax.axis_index("tp")
    plane, place = me >> 2, me & 3


    def section(offset):
        return ((plane + offset[0]) & 7) * PLACES + (place ^ offset[1])

    loads = []
    for b in range(2):
        rows = pl.ds(64 * b, 64)
        for s in range(3):
            loads.append((g_hbm.at[0, s, rows], stage.at[b, s]))
        loads.append((x_hbm.at[0, rows], stage.at[b, 3]))
    loads += [(gain_hbm, gain_v), (w1_hbm.at[0], w1)]
    for b in range(2):
        for f in range(4):
            loads.append((r_hbm.at[0, pl.ds(64 * b, 64), pl.ds(256 * f, 256)], r_stage.at[b, f]))
    loads.append((w2_hbm.at[0], w2.at[pl.ds(0, 96)]))
    loads = [pltpu.make_async_copy(src, dst, in_sem.at[n]) for n, (src, dst) in enumerate(loads)]
    for load in loads[:8]:
        load.start()

    barrier = pltpu.get_barrier_semaphore()

    def greet(device):
        pl.semaphore_signal(barrier, inc=1, device_id=device, device_id_type=MESH)

    for offset in ALL:
        greet({"section": section(offset)})
    for n in range(1, SHARDS):
        greet({"tp": part ^ n})
    for load in loads[8:]:
        load.start()

    class Exchange:
        def __init__(self, peers, here, device, block, landing, ss, rs):
            self.peers, self.here = peers, here

            def copy(to, slot):
                return pltpu.make_async_remote_copy(
                    src_ref=block(to), dst_ref=landing(slot), send_sem=ss.at[to], recv_sem=rs.at[slot],
                    device_id=device(to), device_id_type=MESH,
                )

            self.copy = copy

        def send(self, peers=None):
            for to in peers or self.peers:
                self.copy(to, self.here).start()

        def receive(self):
            for to in self.peers:
                self.copy(to, to).wait_recv()

        def drain(self):
            for to in self.peers:
                self.copy(to, self.here).wait_send()

    by_section = lambda to: {"section": to}
    by_part = lambda to: {"tp": to}
    by_place = lambda to: {"section": plane * PLACES + to}
    by_plane = lambda to: {"section": to * PLACES + place}
    far, middle, close, beside = ([section(offset) for offset in group] for group in (FAR, MIDDLE, CLOSE, NEXT))
    sections = far + middle + close + beside
    parts = [part ^ n for n in AROUND]
    places = [place ^ n for n in range(1, PLACES)]
    planes = [(plane + n) & 7 for n in (4, 3, 5, 2, 6, 1, 7)]
    xg = Exchange(sections, me, by_section, lambda p: sent.at[p], lambda p: held.at[p], x_ss, x_rs)
    wx = Exchange(sections, me, by_section, lambda p: w_sent.at[p], lambda p: w_held.at[p], w_ss, w_rs)
    ox = Exchange(sections, me, by_section, lambda p: o_sent.at[p], lambda p: o_held.at[p], o_ss, o_rs)
    zx = Exchange(parts, part, by_part, lambda p: z_sent.at[p], lambda p: z_held.at[p], z_ss, z_rs)
    ax = Exchange(parts, part, by_part, lambda p: act.at[part], lambda p: act.at[p], a_ss, a_rs)
    dx = Exchange(parts, part, by_part, lambda p: d_sent.at[p], lambda p: d_held.at[p], d_ss, d_rs)
    rx = Exchange(places, place, by_place, lambda p: r_sent.at[:, p], lambda p: r_held.at[p], r_ss, r_rs)
    cx = Exchange(places, place, by_place, lambda p: c_sent.at[p], lambda p: c_held.at[:, p], c_ss, c_rs)
    sx = Exchange(planes, plane, by_plane, lambda p: s_sent.at[p], lambda p: s_held.at[p], s_ss, s_rs)

    row, col = grid(256, 256)
    regroup = pick(((row >> 2) & 3) * 64 + (row >> 4) * 4 + (row & 3) == col)

    for b in range(2):
        for load in loads[4 * b : 4 * b + 4]:
            load.wait()
        grouped = dot(regroup, stage[b].reshape(256, WIDTH)).astype(BF16)
        sent[pl.ds(16 * b, 16)] = grouped.reshape(16, 16, WIDTH)
    loads[8].wait()
    loads[9].wait()
    gain = gain_v[...].astype(F32)
    x = jnp.concatenate([stage[0, 3], stage[1, 3]], axis=0).astype(F32)
    product = dot(jnp.concatenate(halves(x * gain), axis=0), w1[...])
    squares = jnp.broadcast_to(jnp.sum(x * x, axis=1, keepdims=True), (TOKENS, 128))
    z_sent[...] = jnp.concatenate([product[:TOKENS] + product[TOKENS:], squares], axis=1).reshape(SHARDS, 16, 512)

    pl.semaphore_wait(barrier, SECTIONS - 1 + SHARDS - 1)
    zx.send()
    z_held[pl.ds(part, 1)] = z_sent[pl.ds(part, 1)]
    xg.send(far + middle)
    held[pl.ds(me, 1)] = sent[pl.ds(me, 1)]

    for load in loads[10:]:
        load.wait()
    for b in range(2):
        grouped = dot(regroup, r_stage[b].reshape(256, 256)).astype(BF16)
        r_sent[pl.ds(4 * b, 4)] = grouped.reshape(4, PLACES, 16, 256)
    rx.send()
    r_held[pl.ds(place, 1)] = r_sent[:, pl.ds(place, 1)].reshape(1, PLANES, 16, 256)

    zx.receive()
    total = z_held[0]
    for p in range(1, SHARDS):
        total = total + z_held[p]
    scale = lax.rsqrt(total[:, HIDDEN:] / FULL_WIDTH + 1e-05)
    own = jnp.concatenate([total[:, :HIDDEN] * scale[:, :1], scale], axis=1)
    act[pl.ds(part, 1)] = own.reshape(1, 16, 512)
    ax.send()
    xg.send(close + beside)

    rx.receive()
    running = jnp.zeros((PLANES, 16, 256), F32)
    for p in reversed(range(PLACES)):
        running = running + r_held[p].astype(F32)
        c_sent[p] = running.astype(BF16)
    s_sent[...] = running.astype(BF16)
    c_held[:, pl.ds(place, 1)] = c_sent[pl.ds(place, 1)].reshape(PLANES, 1, 16, 256)
    s_held[pl.ds(plane, 1)] = s_sent[pl.ds(plane, 1)]
    cx.send()

    w2[pl.ds(96, 32)] = jnp.zeros((32, HIDDEN), BF16)
    ax.receive()
    pre = act[:, :, :HIDDEN].reshape(TOKENS, HIDDEN)
    inverse = act[:, :, HIDDEN:].reshape(TOKENS, 128)[:, :1]
    square = pre * pre
    bend = jnp.tanh(C0 * pre * (1.0 + C1 * square))
    hidden = 0.5 * pre * (1.0 + bend)
    slope = 0.5 * (1.0 + bend) + 0.5 * pre * (1.0 - bend * bend) * (C0 * (1.0 + 3.0 * C1 * square))
    h_high, h_low = halves(hidden)
    mixing = dot_nt(h_high, w2[...]) + dot_nt(h_low, w2[...])
    row, col = grid(TOKENS, 128)
    mixing = jnp.where((col & 31) <= me, mixing, 0.0)
    w_sent[...] = mixing.reshape(SECTIONS, 4, 128)
    w_held[pl.ds(me, 1)] = w_sent[pl.ds(me, 1)]
    wx.send()
    sx.send()

    row, col = grid(128, 512)
    sel_m[...] = pick((row >> 2) * 16 + 12 + (row & 3) == col)
    fold_m[...] = pick((((row >> 2) & 3) * SHARDS + (row >> 4) == (col >> 4)) & ((row & 3) == (col & 3)))
    wide_m[...] = pick(((row >> 5) == (col >> 7)) & ((row & 31) == ((col >> 2) & 31)))
    row, col = grid(512, 128)
    same = (row & 3) == (col & 3)
    spread_m[...] = pick(((row >> 4) == (col >> 2)) & same)
    same_m[...] = jnp.where(same, 1.0, 0.0)
    which = (row >> 2) & 3
    kept_m[...] = jnp.where((which == (col >> 5)) & (which < 3) & ((col & 31) <= (row >> 4)), 1.0, 0.0)
    row, col = grid(128, 128)
    across_m[...] = pick((row >> 2) == (col & 31))
    row, col = grid(256, 256)
    ungroup_m[...] = pick(((col >> 2) & 3) * 64 + (col >> 4) * 4 + (col & 3) == row)
    for b in range(2):
        x = stage[b, 3].astype(F32)
        normed = (x * inverse[64 * b : 64 * b + 64] * gain).astype(BF16)
        normed_t[:, pl.ds(64 * b, 64)] = normed.T

    xg.receive()
    table = held[...].reshape(512, WIDTH)
    streams = dot(sel_m[...], table).astype(BF16)
    gram = dot_nt(table, streams)
    high, low = halves(gram * same_m[...])
    wide = (dot(high, across_m[...]) + dot(low, across_m[...])) * kept_m[...]
    high, low = halves(wide)
    d_sent[...] = (dot(fold_m[...], high) + dot(fold_m[...], low)).reshape(SHARDS, 16, 128)
    dx.send()
    d_held[pl.ds(part, 1)] = d_sent[pl.ds(part, 1)]

    wx.receive()
    mixing = w_held[...].reshape(128, 128).astype(BF16)
    mixing = dot(spread_m[...], dot(mixing, wide_m[...]).astype(BF16))
    row, col = grid(512, 128)
    which = (row >> 2) & 3
    weights = jnp.where(which == 0, mixing[:, :128], jnp.where(which == 1, mixing[:, 128:256], mixing[:, 256:384]))
    weights = jnp.where(which < 3, weights * same_m[...], 0.0)
    weights = weights.astype(BF16).T
    partial = [dot(weights, table[:, 256 * f : 256 * f + 256]) for f in range(4)]
    sx.receive()
    running = jnp.zeros((16, 256), F32)
    carried = [None] * PLANES
    for p in reversed(range(PLANES)):
        carried[p] = jnp.concatenate([running] * PLACES, axis=0)
        running = running + s_held[p].astype(F32)
    for b in range(2):
        stacked = jnp.concatenate([p[64 * b : 64 * b + 64] for p in partial], axis=0)
        block = dot(regroup, stacked.astype(BF16)) + jnp.concatenate(carried[4 * b : 4 * b + 4], axis=0)
        o_sent[pl.ds(16 * b, 16)] = block.astype(BF16).reshape(16, 16, 256)
    o_held[pl.ds(me, 1)] = o_sent[pl.ds(me, 1)]

    ox.send(far + middle)
    dx.receive()
    total = d_held[0]
    for p in range(1, SHARDS):
        total = total + d_held[p]
    for a in range(4):
        e_sent[a] = total[4 * a : 4 * a + 4]

    home, turn = me & 7, me >> 3

    def e_copy(a, b):
        return pltpu.make_async_remote_copy(
            src_ref=e_sent.at[a], dst_ref=e_held.at[me], send_sem=e_ss.at[a, b], recv_sem=e_rs.at[me],
            device_id={"section": SHARDS * a + part, "tp": b}, device_id_type=MESH,
        )

    def e_each(do):
        for a in (2, 1, 3, 0):
            for n in AROUND:
                do(e_copy((turn + a) & 3, part ^ n))
        for a in range(4):

            @pl.when((home != part) | (turn != a))
            def _():
                do(e_copy(a, part))

    def e_receive(n):
        pltpu.make_async_remote_copy(
            src_ref=e_sent.at[0], dst_ref=e_held.at[n], send_sem=e_ss.at[0, 0], recv_sem=e_rs.at[n],
            device_id={"section": n, "tp": home}, device_id_type=MESH,
        ).wait_recv()

    e_each(lambda copy: copy.start())
    ox.send(close + beside)

    @pl.when(home == part)
    def _():
        e_held[pl.ds(me, 1)] = e_sent[pl.ds(turn, 1)]

    cx.receive()
    near = [dot(ungroup_m[...], c_held[pl.ds(4 * b, 4)].reshape(256, 256)) for b in range(2)]
    for exchange in (zx, ax, rx, cx, sx, xg, wx, dx):
        exchange.drain()

    for n in sections:
        e_receive(n)

    @pl.when(home != part)
    def _():
        e_receive(me)

    mix_grad = e_held[...].reshape(TOKENS, 128)
    g_high, g_low = halves(mix_grad)
    pre_grad = ((dot(g_high, w2[...]) + dot(g_low, w2[...])) * slope).astype(BF16)
    first_v[0] = dot(normed_t[...], pre_grad)
    second = dot_tn(g_high, h_high) + dot_tn(g_low, h_high) + dot_tn(g_high, h_low)
    second_v[0] = second[:96]
    along = jnp.sum(pre_grad.astype(F32) * pre, axis=1, keepdims=True)
    inner = inverse * inverse * along / FULL_WIDTH
    local = inverse * (dot_nt(pre_grad, w1[...]) * gain)

    e_each(lambda copy: copy.wait_send())
    ox.drain()
    ox.receive()
    for b in range(2):
        rows = slice(64 * b, 64 * b + 64)
        arrived = dot(ungroup_m[...], o_held[pl.ds(16 * b, 16)].reshape(256, 256)) + near[b]
        x = stage[b, 3].astype(F32)
        for f in range(4):
            lanes = slice(256 * f, 256 * f + 256)
            value = arrived[64 * f : 64 * f + 64] + (local[rows, lanes] - x[:, lanes] * inner[rows])
            out_v[0, pl.ds(64 * b, 64), pl.ds(256 * f, 256)] = value.astype(BF16)


def handover(out_in, first_in, second_in, out, first, second, sems):
    pairs = ((first_in, first), (out_in, out), (second_in, second))
    copies = [pltpu.make_async_copy(src, dst, sems.at[n]) for n, (src, dst) in enumerate(pairs)]
    for copy in copies:
        copy.start()
    for copy in copies:
        copy.wait()


def local(layer_outputs, stream_grads, residual_grads, norm_gain, first_weight, second_weight):
    hbm = pl.BlockSpec(memory_space=pltpu.HBM)
    vmem = pl.BlockSpec(memory_space=pltpu.VMEM)
    dma = pltpu.SemaphoreType.DMA
    by_section = lambda rows, lanes, dtype: pltpu.VMEM((SECTIONS, rows, lanes), dtype)
    by_part = lambda rows, lanes: pltpu.VMEM((SHARDS, rows, lanes), F32)
    by_place = lambda *lead: pltpu.VMEM((*lead, 16, 256), BF16)
    shapes = (
        jax.ShapeDtypeStruct((1, TOKENS, WIDTH), BF16),
        jax.ShapeDtypeStruct((1, WIDTH, HIDDEN), F32),
        jax.ShapeDtypeStruct((1, 96, HIDDEN), F32),
    )
    args = (layer_outputs, stream_grads, residual_grads, norm_gain, first_weight, jnp.swapaxes(second_weight, 1, 2))
    grads = pl.pallas_call(
        kernel,
        out_shape=shapes,
        in_specs=[hbm] * 6,
        out_specs=(vmem, vmem, vmem),
        scratch_shapes=[
            pltpu.VMEM((2, 4, 64, WIDTH), BF16),
            pltpu.VMEM((2, 4, 64, 256), BF16),
            pltpu.VMEM((1, WIDTH), BF16),
            pltpu.VMEM((WIDTH, HIDDEN), BF16),
            pltpu.VMEM((128, HIDDEN), BF16),
            pltpu.VMEM((512, 128), BF16),
            pltpu.VMEM((128, 512), BF16),
            pltpu.VMEM((128, 512), BF16),
            pltpu.VMEM((128, 128), BF16),
            pltpu.VMEM((128, 512), BF16),
            pltpu.VMEM((512, 128), F32),
            pltpu.VMEM((512, 128), F32),
            pltpu.VMEM((256, 256), BF16),
            pltpu.VMEM((WIDTH, TOKENS), BF16),
            by_section(16, WIDTH, BF16), by_section(16, WIDTH, BF16),
            by_place(PLANES, PLACES), by_place(PLACES, PLANES),
            by_place(PLACES, PLANES), by_place(PLANES, PLACES),
            by_place(PLANES), by_place(PLANES),
            by_section(4, 128, F32), by_section(4, 128, F32),
            by_section(16, 256, BF16), by_section(16, 256, BF16),
            by_part(16, 512), by_part(16, 512), by_part(16, 512),
            by_part(16, 128), by_part(16, 128),
            pltpu.VMEM((4, 4, 128), F32),
            by_section(4, 128, F32),
            dma((19,)),
            *[dma((SECTIONS,)) for _ in range(6)],
            *[dma((PLANES,)) for _ in range(2)],
            *[dma((SHARDS,)) for _ in range(6)],
            *[dma((PLACES,)) for _ in range(4)],
            dma((4, SHARDS)), dma((SECTIONS,)),
        ],
        compiler_params=pltpu.CompilerParams(
            collective_id=0, has_side_effects=True, vmem_limit_bytes=32 * 1024 * 1024
        ),
    )(*[pltpu.with_memory_space_constraint(a, pltpu.HBM) for a in args])
    grads = pl.pallas_call(
        handover,
        out_shape=shapes,
        in_specs=[vmem] * 3,
        out_specs=(hbm,) * 3,
        scratch_shapes=[dma((3,))],
        compiler_params=pltpu.CompilerParams(vmem_limit_bytes=8 * 1024 * 1024),
    )(*[pltpu.with_memory_space_constraint(g, pltpu.VMEM) for g in grads])
    return grads[0], grads[1], jnp.swapaxes(grads[2], 1, 2)


def solution(mesh):
    placed = (
        P("section", None, "tp"),
        P("section", None, None, "tp"),
        P("section", None, "tp"),
        P("section", "tp"),
        P("section", "tp", None),
        P("section", None, None),
    )
    return jax.shard_map(
        local,
        mesh=mesh,
        in_specs=placed,
        out_specs=(P("section", None, "tp"), P("section", "tp", None), P("section", None, None)),
        check_vma=False,
    )
```

```python
import functools

import jax
import jax.numpy as jnp
from jax import lax
from jax.experimental import pallas as pl
from jax.experimental.pallas import tpu as pltpu
from jax.sharding import PartitionSpec as P

MESH = pl.DeviceIdType.MESH
F32, BF16 = jnp.float32, jnp.bfloat16
SECTIONS, SHARDS = 32, 8
PLANES, PLACES = 8, 4
TOKENS, WIDTH, HIDDEN = 128, 1024, 384
FULL_WIDTH = WIDTH * SHARDS
C0, C1 = 0.7978845608028654, 0.044715
FAR = [(4, q) for q in (2, 3, 0, 1)]
MIDDLE = [(z, q) for q in (2, 3, 0, 1) for z in (3, 5)]
CLOSE = [(z, q) for q in range(PLACES) for z in (2, 6)]
NEXT = [(z, q) for q in range(PLACES) for z in (1, 7)] + [(0, q) for q in range(1, PLACES)]
ALL = FAR + MIDDLE + CLOSE + NEXT
AROUND = (5, 7, 3, 4, 1, 6, 2)


def dot(a, b):
    return jnp.dot(a, b, preferred_element_type=F32)


def dot_nt(a, b):
    return lax.dot_general(a, b, (((1,), (1,)), ((), ())), preferred_element_type=F32)


def dot_tn(a, b):
    return lax.dot_general(a, b, (((0,), (0,)), ((), ())), preferred_element_type=F32)


def halves(v):
    high = v.astype(BF16)
    return high, (v - high.astype(F32)).astype(BF16)


def grid(rows, columns):
    return (
        lax.broadcasted_iota(jnp.int32, (rows, columns), 0),
        lax.broadcasted_iota(jnp.int32, (rows, columns), 1),
    )


def pick(condition):
    return jnp.where(condition, 1.0, 0.0).astype(BF16)


def kernel(
    x_hbm, g_hbm, r_hbm, gain_hbm, w1_hbm, w2_hbm,
    out_v, first_v, second_v,
    stage, r_stage, gain_v, w1, w2, spread_m, sel_m, fold_m, across_m, wide_m, same_m, kept_m, ungroup_m, normed_t,
    sent, held, r_sent, r_held, c_sent, c_held, s_sent, s_held, w_sent, w_held, o_sent, o_held,
    z_sent, z_held, act, d_sent, d_held, e_sent, e_held,
    in_sem, sems,
):
    me = lax.axis_index("section")
    part = lax.axis_index("tp")
    plane, place = me >> 2, me & 3


    def section(offset):
        return ((plane + offset[0]) & 7) * PLACES + (place ^ offset[1])

    def load(src, dst, n):
        return pltpu.make_async_copy(src, dst, in_sem.at[n])

    def landed(whole, sem):
        pltpu.make_async_copy(whole, whole, sem).wait()

    def load_streams():
        for b in range(2):
            rows = pl.ds(64 * b, 64)
            for s in range(3):
                load(g_hbm.at[0, s, rows], stage.at[b, s], b).start()
            load(x_hbm.at[0, rows], stage.at[b, 3], b).start()

    def load_rest():
        load(gain_hbm, gain_v, 2).start()
        load(w1_hbm.at[0], w1, 3).start()
        for b in range(2):
            for f in range(4):
                load(r_hbm.at[0, pl.ds(64 * b, 64), pl.ds(256 * f, 256)], r_stage.at[b, f], 4).start()
        load(w2_hbm.at[0], w2.at[pl.ds(0, 96)], 5).start()

    barrier = pltpu.get_barrier_semaphore()

    def greet(device):
        pl.semaphore_signal(barrier, inc=1, device_id=device, device_id_type=MESH)

    for offset in FAR:
        greet({"section": section(offset)})
    greet({"tp": part ^ 5})
    load_streams()
    for offset in MIDDLE:
        greet({"section": section(offset)})
    for n in AROUND[1:]:
        greet({"tp": part ^ n})
    for offset in CLOSE + NEXT:
        greet({"section": section(offset)})
    load_rest()

    class Exchange:
        def __init__(self, peers, here, device, block, landing, bulk, n):
            self.peers, self.here, self.bulk = peers, here, bulk
            self.ss, self.rs = sems.at[2 * n], sems.at[2 * n + 1]

            def copy(to):
                return pltpu.make_async_remote_copy(
                    src_ref=block(to), dst_ref=landing(here), send_sem=self.ss, recv_sem=self.rs,
                    device_id=device(to), device_id_type=MESH,
                )

            self.copy = copy

        def send(self, peers=None):
            for to in peers or self.peers:
                self.copy(to).start()

        def receive(self):
            landed(self.bulk, self.rs)

        def drain(self):
            landed(self.bulk, self.ss)

    by_section = lambda to: {"section": to}
    by_part = lambda to: {"tp": to}
    by_place = lambda to: {"section": plane * PLACES + to}
    by_plane = lambda to: {"section": to * PLACES + place}
    far, middle, close, beside = ([section(offset) for offset in group] for group in (FAR, MIDDLE, CLOSE, NEXT))
    sections = far + middle + close + beside
    parts = [part ^ n for n in AROUND]
    places = [place ^ n for n in range(1, PLACES)]
    planes = [(plane + n) & 7 for n in (4, 3, 5, 2, 6, 1, 7)]
    xg = Exchange(sections, me, by_section, lambda p: sent.at[p], lambda p: held.at[p], held.at[pl.ds(0, 31)], 0)
    wx = Exchange(sections, me, by_section, lambda p: w_sent.at[p], lambda p: w_held.at[p], w_held.at[pl.ds(0, 31)], 1)
    ox = Exchange(sections, me, by_section, lambda p: o_sent.at[p], lambda p: o_held.at[p], o_held.at[pl.ds(0, 31)], 2)
    zx = Exchange(parts, part, by_part, lambda p: z_sent.at[p], lambda p: z_held.at[p], z_held.at[pl.ds(0, 7)], 3)
    ax = Exchange(parts, part, by_part, lambda p: act.at[part], lambda p: act.at[p], act.at[pl.ds(0, 7)], 4)
    dx = Exchange(parts, part, by_part, lambda p: d_sent.at[p], lambda p: d_held.at[p], d_held.at[pl.ds(0, 7)], 5)
    rx = Exchange(places, place, by_place, lambda p: r_sent.at[:, p], lambda p: r_held.at[p], r_held.at[pl.ds(0, 3)], 6)
    cx = Exchange(places, place, by_place, lambda p: c_sent.at[p], lambda p: c_held.at[:, p], c_sent.at[pl.ds(0, 3)], 7)
    sx = Exchange(planes, plane, by_plane, lambda p: s_sent.at[p], lambda p: s_held.at[p], s_held.at[pl.ds(0, 7)], 8)

    row, col = grid(256, 256)
    regroup = pick(((row >> 2) & 3) * 64 + (row >> 4) * 4 + (row & 3) == col)

    for b in range(2):
        landed(stage.at[b], in_sem.at[b])
        grouped = dot(regroup, stage[b].reshape(256, WIDTH)).astype(BF16)
        sent[pl.ds(16 * b, 16)] = grouped.reshape(16, 16, WIDTH)
    load(gain_hbm, gain_v, 2).wait()
    load(w1_hbm.at[0], w1, 3).wait()
    gain = gain_v[...].astype(F32)
    x = jnp.concatenate([stage[0, 3], stage[1, 3]], axis=0).astype(F32)
    product = dot(jnp.concatenate(halves(x * gain), axis=0), w1[...])
    squares = jnp.broadcast_to(jnp.sum(x * x, axis=1, keepdims=True), (TOKENS, 128))
    z_sent[...] = jnp.concatenate([product[:TOKENS] + product[TOKENS:], squares], axis=1).reshape(SHARDS, 16, 512)

    pl.semaphore_wait(barrier, SECTIONS - 1 + SHARDS - 1)
    zx.send()
    z_held[pl.ds(part, 1)] = z_sent[pl.ds(part, 1)]
    xg.send(middle + far)
    held[pl.ds(me, 1)] = sent[pl.ds(me, 1)]

    landed(r_stage, in_sem.at[4])
    load(w2_hbm.at[0], w2.at[pl.ds(0, 96)], 5).wait()
    for b in range(2):
        grouped = dot(regroup, r_stage[b].reshape(256, 256)).astype(BF16)
        r_sent[pl.ds(4 * b, 4)] = grouped.reshape(4, PLACES, 16, 256)
    rx.send()
    r_held[pl.ds(place, 1)] = r_sent[:, pl.ds(place, 1)].reshape(1, PLANES, 16, 256)

    zx.receive()
    total = z_held[0]
    for p in range(1, SHARDS):
        total = total + z_held[p]
    scale = lax.rsqrt(total[:, HIDDEN:] / FULL_WIDTH + 1e-05)
    own = jnp.concatenate([total[:, :HIDDEN] * scale[:, :1], scale], axis=1)
    act[pl.ds(part, 1)] = own.reshape(1, 16, 512)
    ax.send()
    xg.send(close + beside)

    rx.receive()
    running = jnp.zeros((PLANES, 16, 256), F32)
    for p in reversed(range(PLACES)):
        running = running + r_held[p].astype(F32)
        c_sent[p] = running.astype(BF16)
    s_sent[...] = running.astype(BF16)
    c_held[:, pl.ds(place, 1)] = c_sent[pl.ds(place, 1)].reshape(PLANES, 1, 16, 256)
    s_held[pl.ds(plane, 1)] = s_sent[pl.ds(plane, 1)]
    cx.send()

    w2[pl.ds(96, 32)] = jnp.zeros((32, HIDDEN), BF16)
    ax.receive()
    pre = act[:, :, :HIDDEN].reshape(TOKENS, HIDDEN)
    inverse = act[:, :, HIDDEN:].reshape(TOKENS, 128)[:, :1]
    square = pre * pre
    bend = jnp.tanh(C0 * pre * (1.0 + C1 * square))
    hidden = 0.5 * pre * (1.0 + bend)
    slope = 0.5 * (1.0 + bend) + 0.5 * pre * (1.0 - bend * bend) * (C0 * (1.0 + 3.0 * C1 * square))
    h_high, h_low = halves(hidden)
    mixing = dot_nt(h_high, w2[...]) + dot_nt(h_low, w2[...])
    row, col = grid(TOKENS, 128)
    mixing = jnp.where((col & 31) <= me, mixing, 0.0)
    w_sent[...] = mixing.reshape(SECTIONS, 4, 128)
    w_held[pl.ds(me, 1)] = w_sent[pl.ds(me, 1)]
    wx.send()
    sx.send()

    row, col = grid(128, 512)
    sel_m[...] = pick((row >> 2) * 16 + 12 + (row & 3) == col)
    fold_m[...] = pick((((row >> 2) & 3) * SHARDS + (row >> 4) == (col >> 4)) & ((row & 3) == (col & 3)))
    wide_m[...] = pick(((row >> 5) == (col >> 7)) & ((row & 31) == ((col >> 2) & 31)))
    row, col = grid(512, 128)
    same = (row & 3) == (col & 3)
    spread_m[...] = pick(((row >> 4) == (col >> 2)) & same)
    same_m[...] = jnp.where(same, 1.0, 0.0)
    which = (row >> 2) & 3
    kept_m[...] = jnp.where((which == (col >> 5)) & (which < 3) & ((col & 31) <= (row >> 4)), 1.0, 0.0)
    row, col = grid(128, 128)
    across_m[...] = pick((row >> 2) == (col & 31))
    row, col = grid(256, 256)
    ungroup_m[...] = pick(((col >> 2) & 3) * 64 + (col >> 4) * 4 + (col & 3) == row)
    for b in range(2):
        x = stage[b, 3].astype(F32)
        normed = (x * inverse[64 * b : 64 * b + 64] * gain).astype(BF16)
        normed_t[:, pl.ds(64 * b, 64)] = normed.T

    xg.receive()
    table = held[...].reshape(512, WIDTH)
    streams = dot(sel_m[...], table).astype(BF16)
    gram = dot_nt(table, streams)
    high, low = halves(gram * same_m[...])
    wide = (dot(high, across_m[...]) + dot(low, across_m[...])) * kept_m[...]
    high, low = halves(wide)
    d_sent[...] = (dot(fold_m[...], high) + dot(fold_m[...], low)).reshape(SHARDS, 16, 128)
    dx.send()
    d_held[pl.ds(part, 1)] = d_sent[pl.ds(part, 1)]

    wx.receive()
    mixing = w_held[...].reshape(128, 128).astype(BF16)
    mixing = dot(spread_m[...], dot(mixing, wide_m[...]).astype(BF16))
    row, col = grid(512, 128)
    which = (row >> 2) & 3
    weights = jnp.where(which == 0, mixing[:, :128], jnp.where(which == 1, mixing[:, 128:256], mixing[:, 256:384]))
    weights = jnp.where(which < 3, weights * same_m[...], 0.0)
    weights = weights.astype(BF16).T
    partial = [dot(weights, table[:, 256 * f : 256 * f + 256]) for f in range(4)]
    sx.receive()
    running = jnp.zeros((16, 256), F32)
    carried = [None] * PLANES
    for p in reversed(range(PLANES)):
        carried[p] = jnp.concatenate([running] * PLACES, axis=0)
        running = running + s_held[p].astype(F32)
    for b in range(2):
        stacked = jnp.concatenate([p[64 * b : 64 * b + 64] for p in partial], axis=0)
        block = dot(regroup, stacked.astype(BF16)) + jnp.concatenate(carried[4 * b : 4 * b + 4], axis=0)
        o_sent[pl.ds(16 * b, 16)] = block.astype(BF16).reshape(16, 16, 256)
    o_held[pl.ds(me, 1)] = o_sent[pl.ds(me, 1)]

    ox.send(far + middle)
    dx.receive()
    total = d_held[0]
    for p in range(1, SHARDS):
        total = total + d_held[p]
    for a in range(4):
        e_sent[a] = total[4 * a : 4 * a + 4]

    home, turn = me & 7, me >> 3

    def e_copy(a, b):
        return pltpu.make_async_remote_copy(
            src_ref=e_sent.at[a], dst_ref=e_held.at[me], send_sem=sems.at[18], recv_sem=sems.at[19],
            device_id={"section": SHARDS * a + part, "tp": b}, device_id_type=MESH,
        )

    def e_each(do):
        for a in range(4):
            for n in AROUND:
                do(e_copy(a, part ^ n))

            @pl.when((home != part) | (turn != a))
            def _(a=a):
                do(e_copy(a, part))

    def e_landed(sem):
        @pl.when(home == part)
        def _():
            landed(e_held.at[pl.ds(0, 31)], sem)

        @pl.when(home != part)
        def _():
            landed(e_held, sem)

    e_each(lambda copy: copy.start())
    ox.send(close + beside)

    @pl.when(home == part)
    def _():
        e_held[pl.ds(me, 1)] = e_sent[pl.ds(turn, 1)]

    cx.receive()
    near = [dot(ungroup_m[...], c_held[pl.ds(4 * b, 4)].reshape(256, 256)) for b in range(2)]
    for exchange in (zx, ax, rx, cx, sx, xg, wx, dx):
        exchange.drain()

    e_landed(sems.at[19])

    mix_grad = e_held[...].reshape(TOKENS, 128)
    g_high, g_low = halves(mix_grad)
    pre_grad = ((dot(g_high, w2[...]) + dot(g_low, w2[...])) * slope).astype(BF16)
    first_v[0] = dot(normed_t[...], pre_grad)
    second = dot_tn(g_high, h_high) + dot_tn(g_low, h_high) + dot_tn(g_high, h_low)
    second_v[0] = second[:96]
    along = jnp.sum(pre_grad.astype(F32) * pre, axis=1, keepdims=True)
    inner = inverse * inverse * along / FULL_WIDTH
    local = inverse * (dot_nt(pre_grad, w1[...]) * gain)

    e_landed(sems.at[18])
    ox.drain()
    ox.receive()
    for b in range(2):
        rows = slice(64 * b, 64 * b + 64)
        arrived = dot(ungroup_m[...], o_held[pl.ds(16 * b, 16)].reshape(256, 256)) + near[b]
        x = stage[b, 3].astype(F32)
        for f in range(4):
            lanes = slice(256 * f, 256 * f + 256)
            value = arrived[64 * f : 64 * f + 64] + (local[rows, lanes] - x[:, lanes] * inner[rows])
            out_v[0, pl.ds(64 * b, 64), pl.ds(256 * f, 256)] = value.astype(BF16)


def handover(out_in, first_in, second_in, out, first, second, sems):
    pairs = ((first_in, first), (out_in, out), (second_in, second))
    copies = [pltpu.make_async_copy(src, dst, sems.at[n]) for n, (src, dst) in enumerate(pairs)]
    for copy in copies:
        copy.start()
    for copy in copies:
        copy.wait()


def local(layer_outputs, stream_grads, residual_grads, norm_gain, first_weight, second_weight):
    hbm = pl.BlockSpec(memory_space=pltpu.HBM)
    vmem = pl.BlockSpec(memory_space=pltpu.VMEM)
    dma = pltpu.SemaphoreType.DMA
    by_section = lambda rows, lanes, dtype: pltpu.VMEM((SECTIONS, rows, lanes), dtype)
    by_part = lambda rows, lanes: pltpu.VMEM((SHARDS, rows, lanes), F32)
    by_place = lambda *lead: pltpu.VMEM((*lead, 16, 256), BF16)
    shapes = (
        jax.ShapeDtypeStruct((1, TOKENS, WIDTH), BF16),
        jax.ShapeDtypeStruct((1, WIDTH, HIDDEN), F32),
        jax.ShapeDtypeStruct((1, 96, HIDDEN), F32),
    )
    args = (layer_outputs, stream_grads, residual_grads, norm_gain, first_weight, jnp.swapaxes(second_weight, 1, 2))
    grads = pl.pallas_call(
        kernel,
        out_shape=shapes,
        in_specs=[hbm] * 6,
        out_specs=(vmem, vmem, vmem),
        scratch_shapes=[
            pltpu.VMEM((2, 4, 64, WIDTH), BF16),
            pltpu.VMEM((2, 4, 64, 256), BF16),
            pltpu.VMEM((1, WIDTH), BF16),
            pltpu.VMEM((WIDTH, HIDDEN), BF16),
            pltpu.VMEM((128, HIDDEN), BF16),
            pltpu.VMEM((512, 128), BF16),
            pltpu.VMEM((128, 512), BF16),
            pltpu.VMEM((128, 512), BF16),
            pltpu.VMEM((128, 128), BF16),
            pltpu.VMEM((128, 512), BF16),
            pltpu.VMEM((512, 128), F32),
            pltpu.VMEM((512, 128), F32),
            pltpu.VMEM((256, 256), BF16),
            pltpu.VMEM((WIDTH, TOKENS), BF16),
            by_section(16, WIDTH, BF16), by_section(16, WIDTH, BF16),
            by_place(PLANES, PLACES), by_place(PLACES, PLANES),
            by_place(PLACES, PLANES), by_place(PLANES, PLACES),
            by_place(PLANES), by_place(PLANES),
            by_section(4, 128, F32), by_section(4, 128, F32),
            by_section(16, 256, BF16), by_section(16, 256, BF16),
            by_part(16, 512), by_part(16, 512), by_part(16, 512),
            by_part(16, 128), by_part(16, 128),
            pltpu.VMEM((4, 4, 128), F32),
            by_section(4, 128, F32),
            dma((6,)), dma((20,)),
        ],
        compiler_params=pltpu.CompilerParams(
            collective_id=0, has_side_effects=True, vmem_limit_bytes=32 * 1024 * 1024
        ),
    )(*[pltpu.with_memory_space_constraint(a, pltpu.HBM) for a in args])
    grads = pl.pallas_call(
        handover,
        out_shape=shapes,
        in_specs=[vmem] * 3,
        out_specs=(hbm,) * 3,
        scratch_shapes=[dma((3,))],
        compiler_params=pltpu.CompilerParams(vmem_limit_bytes=8 * 1024 * 1024),
    )(*[pltpu.with_memory_space_constraint(g, pltpu.VMEM) for g in grads])
    return grads[0], grads[1], jnp.swapaxes(grads[2], 1, 2)


def solution(mesh):
    placed = (
        P("section", None, "tp"),
        P("section", None, None, "tp"),
        P("section", None, "tp"),
        P("section", "tp"),
        P("section", "tp", None),
        P("section", None, None),
    )
    return jax.shard_map(
        local,
        mesh=mesh,
        in_specs=placed,
        out_specs=(P("section", None, "tp"), P("section", "tp", None), P("section", None, None)),
        check_vma=False,
    )
```

```python
import functools

import jax
import jax.numpy as jnp
from jax import lax
from jax.experimental import pallas as pl
from jax.experimental.pallas import tpu as pltpu
from jax.sharding import PartitionSpec as P

MESH = pl.DeviceIdType.MESH
F32, BF16 = jnp.float32, jnp.bfloat16
SECTIONS, SHARDS = 32, 8
PLANES, PLACES = 8, 4
PIECES = 4
TOKENS, WIDTH, HIDDEN = 128, 1024, 384
FULL_WIDTH = WIDTH * SHARDS
C0, C1 = 0.7978845608028654, 0.044715
FAR = [(4, q) for q in (2, 3, 0, 1)]
MIDDLE = [(z, q) for q in (2, 3, 0, 1) for z in (3, 5)]
CLOSE = [(z, q) for q in range(PLACES) for z in (2, 6)]
NEXT = [(z, q) for q in range(PLACES) for z in (1, 7)] + [(0, q) for q in range(1, PLACES)]
ALL = FAR + MIDDLE + CLOSE + NEXT
AROUND = (5, 7, 3, 4, 1, 6, 2)


def dot(a, b):
    return jnp.dot(a, b, preferred_element_type=F32)


def dot_nt(a, b):
    return lax.dot_general(a, b, (((1,), (1,)), ((), ())), preferred_element_type=F32)


def dot_tn(a, b):
    return lax.dot_general(a, b, (((0,), (0,)), ((), ())), preferred_element_type=F32)


def halves(v):
    high = v.astype(BF16)
    return high, (v - high.astype(F32)).astype(BF16)


def grid(rows, columns):
    return (
        lax.broadcasted_iota(jnp.int32, (rows, columns), 0),
        lax.broadcasted_iota(jnp.int32, (rows, columns), 1),
    )


def pick(condition):
    return jnp.where(condition, 1.0, 0.0).astype(BF16)


def kernel(
    x_hbm, g_hbm, r_hbm, gain_hbm, w1_hbm, w2_hbm,
    out_v, normed_t, pre_v, second_v,
    stage, r_stage, gain_v, w1, w2, spread_m, sel_m, fold_m, across_m, wide_m, same_m, kept_m, ungroup_m,
    sent, held, r_sent, r_held, c_sent, c_held, s_sent, s_held, w_sent, w_held, o_sent, o_held,
    z_sent, z_held, act, d_sent, d_held, e_sent, e_held,
    in_sem, sems,
):
    me = lax.axis_index("section")
    part = lax.axis_index("tp")
    plane, place = me >> 2, me & 3


    def section(offset):
        return ((plane + offset[0]) & 7) * PLACES + (place ^ offset[1])

    def load(src, dst, n):
        return pltpu.make_async_copy(src, dst, in_sem.at[n])

    def landed(whole, sem):
        pltpu.make_async_copy(whole, whole, sem).wait()

    def load_streams():
        for b in range(2):
            rows = pl.ds(64 * b, 64)
            for s in range(3):
                load(g_hbm.at[0, s, rows], stage.at[b, s], b).start()
            load(x_hbm.at[0, rows], stage.at[b, 3], b).start()

    def load_rest():
        load(gain_hbm, gain_v, 2).start()
        load(w1_hbm.at[0], w1, 3).start()
        for b in range(2):
            for f in range(4):
                load(r_hbm.at[0, pl.ds(64 * b, 64), pl.ds(256 * f, 256)], r_stage.at[b, f], 4).start()
        load(w2_hbm.at[0], w2.at[pl.ds(0, 96)], 5).start()

    barrier = pltpu.get_barrier_semaphore()

    def greet(device):
        pl.semaphore_signal(barrier, inc=1, device_id=device, device_id_type=MESH)

    for offset in FAR:
        greet({"section": section(offset)})
    greet({"tp": part ^ 5})
    load_streams()
    for offset in MIDDLE:
        greet({"section": section(offset)})
    for n in AROUND[1:]:
        greet({"tp": part ^ n})
    for offset in CLOSE + NEXT:
        greet({"section": section(offset)})
    load_rest()

    class Exchange:
        def __init__(self, peers, here, device, block, landing, bulk, n):
            self.peers, self.here, self.bulk = peers, here, bulk
            self.ss, self.rs = sems.at[2 * n], sems.at[2 * n + 1]

            def copy(to):
                return pltpu.make_async_remote_copy(
                    src_ref=block(to), dst_ref=landing(here), send_sem=self.ss, recv_sem=self.rs,
                    device_id=device(to), device_id_type=MESH,
                )

            self.copy = copy

        def send(self, peers=None):
            for to in peers or self.peers:
                self.copy(to).start()

        def receive(self):
            landed(self.bulk, self.rs)

        def drain(self):
            landed(self.bulk, self.ss)

    by_section = lambda to: {"section": to}
    by_part = lambda to: {"tp": to}
    by_place = lambda to: {"section": plane * PLACES + to}
    by_plane = lambda to: {"section": to * PLACES + place}
    far, middle, close, beside = ([section(offset) for offset in group] for group in (FAR, MIDDLE, CLOSE, NEXT))
    sections = far + middle + close + beside
    parts = [part ^ n for n in AROUND]
    places = [place ^ n for n in range(1, PLACES)]
    planes = [(plane + n) & 7 for n in (4, 3, 5, 2, 6, 1, 7)]
    xg = Exchange(sections, me, by_section, lambda p: sent.at[p], lambda p: held.at[p], held.at[pl.ds(0, 31)], 0)
    wx = Exchange(sections, me, by_section, lambda p: w_sent.at[p], lambda p: w_held.at[p], w_held.at[pl.ds(0, 31)], 1)
    ox = Exchange(sections, me, by_section, lambda p: o_sent.at[p], lambda p: o_held.at[p], o_held.at[pl.ds(0, 31)], 2)
    zx = Exchange(parts, part, by_part, lambda p: z_sent.at[p], lambda p: z_held.at[p], z_held.at[pl.ds(0, 7)], 3)
    ax = Exchange(parts, part, by_part, lambda p: act.at[part], lambda p: act.at[p], act.at[pl.ds(0, 7)], 4)
    dx = Exchange(parts, part, by_part, lambda p: d_sent.at[p], lambda p: d_held.at[p], d_held.at[pl.ds(0, 7)], 5)
    rx = Exchange(places, place, by_place, lambda p: r_sent.at[:, p], lambda p: r_held.at[p], r_held.at[pl.ds(0, 3)], 6)
    cx = Exchange(places, place, by_place, lambda p: c_sent.at[p], lambda p: c_held.at[:, p], c_sent.at[pl.ds(0, 3)], 7)
    sx = Exchange(planes, plane, by_plane, lambda p: s_sent.at[p], lambda p: s_held.at[p], s_held.at[pl.ds(0, 7)], 8)

    row, col = grid(256, 256)
    regroup = pick(((row >> 2) & 3) * 64 + (row >> 4) * 4 + (row & 3) == col)

    for b in range(2):
        landed(stage.at[b], in_sem.at[b])
        grouped = dot(regroup, stage[b].reshape(256, WIDTH)).astype(BF16)
        sent[pl.ds(16 * b, 16)] = grouped.reshape(16, 16, WIDTH)
    load(gain_hbm, gain_v, 2).wait()
    load(w1_hbm.at[0], w1, 3).wait()
    gain = gain_v[...].astype(F32)
    x = jnp.concatenate([stage[0, 3], stage[1, 3]], axis=0).astype(F32)
    product = dot(jnp.concatenate(halves(x * gain), axis=0), w1[...])
    squares = jnp.broadcast_to(jnp.sum(x * x, axis=1, keepdims=True), (TOKENS, 128))
    z_sent[...] = jnp.concatenate([product[:TOKENS] + product[TOKENS:], squares], axis=1).reshape(SHARDS, 16, 512)

    pl.semaphore_wait(barrier, SECTIONS - 1 + SHARDS - 1)
    zx.send()
    z_held[pl.ds(part, 1)] = z_sent[pl.ds(part, 1)]
    xg.send(middle + far)
    held[pl.ds(me, 1)] = sent[pl.ds(me, 1)]

    landed(r_stage, in_sem.at[4])
    load(w2_hbm.at[0], w2.at[pl.ds(0, 96)], 5).wait()
    for b in range(2):
        grouped = dot(regroup, r_stage[b].reshape(256, 256)).astype(BF16)
        r_sent[pl.ds(4 * b, 4)] = grouped.reshape(4, PLACES, 16, 256)
    rx.send()
    r_held[pl.ds(place, 1)] = r_sent[:, pl.ds(place, 1)].reshape(1, PLANES, 16, 256)

    zx.receive()
    total = z_held[0]
    for p in range(1, SHARDS):
        total = total + z_held[p]
    scale = lax.rsqrt(total[:, HIDDEN:] / FULL_WIDTH + 1e-05)
    own = jnp.concatenate([total[:, :HIDDEN] * scale[:, :1], scale], axis=1)
    act[pl.ds(part, 1)] = own.reshape(1, 16, 512)
    ax.send()
    xg.send(close + beside)

    rx.receive()
    running = jnp.zeros((PLANES, 16, 256), F32)
    for p in reversed(range(PLACES)):
        running = running + r_held[p].astype(F32)
        c_sent[p] = running.astype(BF16)
    s_sent[...] = running.astype(BF16)
    c_held[:, pl.ds(place, 1)] = c_sent[pl.ds(place, 1)].reshape(PLANES, 1, 16, 256)
    s_held[pl.ds(plane, 1)] = s_sent[pl.ds(plane, 1)]
    cx.send()

    w2[pl.ds(96, 32)] = jnp.zeros((32, HIDDEN), BF16)
    ax.receive()
    pre = act[:, :, :HIDDEN].reshape(TOKENS, HIDDEN)
    inverse = act[:, :, HIDDEN:].reshape(TOKENS, 128)[:, :1]
    square = pre * pre
    bend = jnp.tanh(C0 * pre * (1.0 + C1 * square))
    hidden = 0.5 * pre * (1.0 + bend)
    slope = 0.5 * (1.0 + bend) + 0.5 * pre * (1.0 - bend * bend) * (C0 * (1.0 + 3.0 * C1 * square))
    h_high, h_low = halves(hidden)
    mixing = dot_nt(h_high, w2[...]) + dot_nt(h_low, w2[...])
    row, col = grid(TOKENS, 128)
    mixing = jnp.where((col & 31) <= me, mixing, 0.0)
    w_sent[...] = mixing.reshape(SECTIONS, 4, 128)
    w_held[pl.ds(me, 1)] = w_sent[pl.ds(me, 1)]
    wx.send()
    sx.send()

    row, col = grid(128, 512)
    sel_m[...] = pick((row >> 2) * 16 + 12 + (row & 3) == col)
    fold_m[...] = pick((((row >> 2) & 3) * SHARDS + (row >> 4) == (col >> 4)) & ((row & 3) == (col & 3)))
    wide_m[...] = pick(((row >> 5) == (col >> 7)) & ((row & 31) == ((col >> 2) & 31)))
    row, col = grid(512, 128)
    same = (row & 3) == (col & 3)
    spread_m[...] = pick(((row >> 4) == (col >> 2)) & same)
    same_m[...] = jnp.where(same, 1.0, 0.0)
    which = (row >> 2) & 3
    kept_m[...] = jnp.where((which == (col >> 5)) & (which < 3) & ((col & 31) <= (row >> 4)), 1.0, 0.0)
    row, col = grid(128, 128)
    across_m[...] = pick((row >> 2) == (col & 31))
    row, col = grid(256, 256)
    ungroup_m[...] = pick(((col >> 2) & 3) * 64 + (col >> 4) * 4 + (col & 3) == row)
    for b in range(2):
        x = stage[b, 3].astype(F32)
        normed = (x * inverse[64 * b : 64 * b + 64] * gain).astype(BF16)
        normed_t[:, pl.ds(64 * b, 64)] = normed.T

    xg.receive()
    table = held[...].reshape(512, WIDTH)
    streams = dot(sel_m[...], table).astype(BF16)
    gram = dot_nt(table, streams)
    high, low = halves(gram * same_m[...])
    wide = (dot(high, across_m[...]) + dot(low, across_m[...])) * kept_m[...]
    high, low = halves(wide)
    d_sent[...] = (dot(fold_m[...], high) + dot(fold_m[...], low)).reshape(SHARDS, 16, 128)
    dx.send()
    d_held[pl.ds(part, 1)] = d_sent[pl.ds(part, 1)]

    wx.receive()
    mixing = w_held[...].reshape(128, 128).astype(BF16)
    mixing = dot(spread_m[...], dot(mixing, wide_m[...]).astype(BF16))
    row, col = grid(512, 128)
    which = (row >> 2) & 3
    weights = jnp.where(which == 0, mixing[:, :128], jnp.where(which == 1, mixing[:, 128:256], mixing[:, 256:384]))
    weights = jnp.where(which < 3, weights * same_m[...], 0.0)
    weights = weights.astype(BF16).T
    partial = [dot(weights, table[:, 256 * f : 256 * f + 256]) for f in range(4)]
    sx.receive()
    running = jnp.zeros((16, 256), F32)
    carried = [None] * PLANES
    for p in reversed(range(PLANES)):
        carried[p] = jnp.concatenate([running] * PLACES, axis=0)
        running = running + s_held[p].astype(F32)
    for b in range(2):
        stacked = jnp.concatenate([p[64 * b : 64 * b + 64] for p in partial], axis=0)
        block = dot(regroup, stacked.astype(BF16)) + jnp.concatenate(carried[4 * b : 4 * b + 4], axis=0)
        o_sent[pl.ds(16 * b, 16)] = block.astype(BF16).reshape(16, 16, 256)
    o_held[pl.ds(me, 1)] = o_sent[pl.ds(me, 1)]

    ox.send(far + middle)
    dx.receive()
    total = d_held[0]
    for p in range(1, SHARDS):
        total = total + d_held[p]
    for a in range(4):
        e_sent[a] = total[4 * a : 4 * a + 4]

    home, turn = me & 7, me >> 3

    def e_copy(a, b):
        return pltpu.make_async_remote_copy(
            src_ref=e_sent.at[a], dst_ref=e_held.at[me], send_sem=sems.at[18], recv_sem=sems.at[19],
            device_id={"section": SHARDS * a + part, "tp": b}, device_id_type=MESH,
        )

    def e_each(do):
        for a in range(4):
            for n in AROUND:
                do(e_copy(a, part ^ n))

            @pl.when((home != part) | (turn != a))
            def _(a=a):
                do(e_copy(a, part))

    def e_landed(sem):
        @pl.when(home == part)
        def _():
            landed(e_held.at[pl.ds(0, 31)], sem)

        @pl.when(home != part)
        def _():
            landed(e_held, sem)

    e_each(lambda copy: copy.start())
    ox.send(close + beside)

    @pl.when(home == part)
    def _():
        e_held[pl.ds(me, 1)] = e_sent[pl.ds(turn, 1)]

    cx.receive()
    near = [dot(ungroup_m[...], c_held[pl.ds(4 * b, 4)].reshape(256, 256)) for b in range(2)]
    for exchange in (zx, ax, rx, cx, sx, xg, wx, dx):
        exchange.drain()

    e_landed(sems.at[19])

    mix_grad = e_held[...].reshape(TOKENS, 128)
    g_high, g_low = halves(mix_grad)
    pre_grad = ((dot(g_high, w2[...]) + dot(g_low, w2[...])) * slope).astype(BF16)
    pre_v[...] = pre_grad
    second = dot_tn(g_high, h_high) + dot_tn(g_low, h_high) + dot_tn(g_high, h_low)
    second_v[0] = second[:96]
    along = jnp.sum(pre_grad.astype(F32) * pre, axis=1, keepdims=True)
    inner = inverse * inverse * along / FULL_WIDTH
    local = inverse * (dot_nt(pre_grad, w1[...]) * gain)

    e_landed(sems.at[18])
    ox.drain()
    ox.receive()
    for b in range(2):
        rows = slice(64 * b, 64 * b + 64)
        arrived = dot(ungroup_m[...], o_held[pl.ds(16 * b, 16)].reshape(256, 256)) + near[b]
        x = stage[b, 3].astype(F32)
        for f in range(4):
            lanes = slice(256 * f, 256 * f + 256)
            value = arrived[64 * f : 64 * f + 64] + (local[rows, lanes] - x[:, lanes] * inner[rows])
            out_v[0, pl.ds(64 * b, 64), pl.ds(256 * f, 256)] = value.astype(BF16)


def handover(out_in, normed_t, pre_grad, second_in, out, first, second, first_v, sems):
    copies = [
        pltpu.make_async_copy(out_in, out, sems.at[0]),
        pltpu.make_async_copy(second_in, second, sems.at[1]),
    ]
    for copy in copies:
        copy.start()
    step = WIDTH // PIECES
    for n in range(PIECES):
        rows = pl.ds(step * n, step)
        first_v[rows] = dot(normed_t[rows], pre_grad[...])
        copies.append(pltpu.make_async_copy(first_v.at[rows], first.at[0, rows], sems.at[2 + n]))
        copies[-1].start()
    for copy in copies:
        copy.wait()


def local(layer_outputs, stream_grads, residual_grads, norm_gain, first_weight, second_weight):
    hbm = pl.BlockSpec(memory_space=pltpu.HBM)
    vmem = pl.BlockSpec(memory_space=pltpu.VMEM)
    dma = pltpu.SemaphoreType.DMA
    by_section = lambda rows, lanes, dtype: pltpu.VMEM((SECTIONS, rows, lanes), dtype)
    by_part = lambda rows, lanes: pltpu.VMEM((SHARDS, rows, lanes), F32)
    by_place = lambda *lead: pltpu.VMEM((*lead, 16, 256), BF16)
    shapes = (
        jax.ShapeDtypeStruct((1, TOKENS, WIDTH), BF16),
        jax.ShapeDtypeStruct((1, WIDTH, HIDDEN), F32),
        jax.ShapeDtypeStruct((1, 96, HIDDEN), F32),
    )
    args = (layer_outputs, stream_grads, residual_grads, norm_gain, first_weight, jnp.swapaxes(second_weight, 1, 2))
    grads = pl.pallas_call(
        kernel,
        out_shape=(
            shapes[0],
            jax.ShapeDtypeStruct((WIDTH, TOKENS), BF16),
            jax.ShapeDtypeStruct((TOKENS, HIDDEN), BF16),
            shapes[2],
        ),
        in_specs=[hbm] * 6,
        out_specs=(vmem,) * 4,
        scratch_shapes=[
            pltpu.VMEM((2, 4, 64, WIDTH), BF16),
            pltpu.VMEM((2, 4, 64, 256), BF16),
            pltpu.VMEM((1, WIDTH), BF16),
            pltpu.VMEM((WIDTH, HIDDEN), BF16),
            pltpu.VMEM((128, HIDDEN), BF16),
            pltpu.VMEM((512, 128), BF16),
            pltpu.VMEM((128, 512), BF16),
            pltpu.VMEM((128, 512), BF16),
            pltpu.VMEM((128, 128), BF16),
            pltpu.VMEM((128, 512), BF16),
            pltpu.VMEM((512, 128), F32),
            pltpu.VMEM((512, 128), F32),
            pltpu.VMEM((256, 256), BF16),
            by_section(16, WIDTH, BF16), by_section(16, WIDTH, BF16),
            by_place(PLANES, PLACES), by_place(PLACES, PLANES),
            by_place(PLACES, PLANES), by_place(PLANES, PLACES),
            by_place(PLANES), by_place(PLANES),
            by_section(4, 128, F32), by_section(4, 128, F32),
            by_section(16, 256, BF16), by_section(16, 256, BF16),
            by_part(16, 512), by_part(16, 512), by_part(16, 512),
            by_part(16, 128), by_part(16, 128),
            pltpu.VMEM((4, 4, 128), F32),
            by_section(4, 128, F32),
            dma((6,)), dma((20,)),
        ],
        compiler_params=pltpu.CompilerParams(
            collective_id=0, has_side_effects=True, vmem_limit_bytes=32 * 1024 * 1024
        ),
    )(*[pltpu.with_memory_space_constraint(a, pltpu.HBM) for a in args])
    grads = pl.pallas_call(
        handover,
        out_shape=shapes,
        in_specs=[vmem] * 4,
        out_specs=(hbm,) * 3,
        scratch_shapes=[pltpu.VMEM((WIDTH, HIDDEN), F32), dma((PIECES + 2,))],
        compiler_params=pltpu.CompilerParams(vmem_limit_bytes=8 * 1024 * 1024),
    )(*[pltpu.with_memory_space_constraint(g, pltpu.VMEM) for g in grads])
    return grads[0], grads[1], jnp.swapaxes(grads[2], 1, 2)


def solution(mesh):
    placed = (
        P("section", None, "tp"),
        P("section", None, None, "tp"),
        P("section", None, "tp"),
        P("section", "tp"),
        P("section", "tp", None),
        P("section", None, None),
    )
    return jax.shard_map(
        local,
        mesh=mesh,
        in_specs=placed,
        out_specs=(P("section", None, "tp"), P("section", "tp", None), P("section", None, None)),
        check_vma=False,
    )
```

```python
import functools

import jax
import jax.numpy as jnp
from jax import lax
from jax.experimental import pallas as pl
from jax.experimental.pallas import tpu as pltpu
from jax.sharding import PartitionSpec as P

MESH = pl.DeviceIdType.MESH
F32, BF16 = jnp.float32, jnp.bfloat16
SECTIONS, SHARDS = 32, 8
PLANES, PLACES = 8, 4
TOKENS, WIDTH, HIDDEN = 128, 1024, 384
FULL_WIDTH = WIDTH * SHARDS
C0, C1 = 0.7978845608028654, 0.044715
FAR = [(4, q) for q in (2, 3, 0, 1)]
MIDDLE = [(z, q) for q in (2, 3, 0, 1) for z in (3, 5)]
CLOSE = [(z, q) for q in range(PLACES) for z in (2, 6)]
NEXT = [(z, q) for q in range(PLACES) for z in (1, 7)] + [(0, q) for q in range(1, PLACES)]
ALL = FAR + MIDDLE + CLOSE + NEXT
AROUND = (5, 7, 3, 4, 1, 6, 2)


def dot(a, b):
    return jnp.dot(a, b, preferred_element_type=F32)


def dot_nt(a, b):
    return lax.dot_general(a, b, (((1,), (1,)), ((), ())), preferred_element_type=F32)


def dot_tn(a, b):
    return lax.dot_general(a, b, (((0,), (0,)), ((), ())), preferred_element_type=F32)


def halves(v):
    high = v.astype(BF16)
    return high, (v - high.astype(F32)).astype(BF16)


def grid(rows, columns):
    return (
        lax.broadcasted_iota(jnp.int32, (rows, columns), 0),
        lax.broadcasted_iota(jnp.int32, (rows, columns), 1),
    )


def pick(condition):
    return jnp.where(condition, 1.0, 0.0).astype(BF16)


def kernel(
    x_hbm, g_hbm, r_hbm, gain_hbm, w1_hbm, w2_hbm,
    out_v, first_v, second_v,
    stage, r_stage, gain_v, w1, w2, spread_m, sel_m, fold_m, across_m, wide_m, same_m, kept_m, ungroup_m, normed_t,
    sent, held, r_sent, r_held, c_sent, c_held, s_sent, s_held, w_sent, w_held, o_sent, o_held,
    z_sent, z_held, act, d_sent, d_held, e_sent, e_held,
    in_sem, sems,
):
    me = lax.axis_index("section")
    part = lax.axis_index("tp")
    plane, place = me >> 2, me & 3


    def section(offset):
        return ((plane + offset[0]) & 7) * PLACES + (place ^ offset[1])

    def load(src, dst, n):
        return pltpu.make_async_copy(src, dst, in_sem.at[n])

    def landed(whole, sem):
        pltpu.make_async_copy(whole, whole, sem).wait()

    def load_streams():
        for b in range(2):
            rows = pl.ds(64 * b, 64)
            for s in range(3):
                load(g_hbm.at[0, s, rows], stage.at[b, s], b).start()
            load(x_hbm.at[0, rows], stage.at[b, 3], b).start()

    def load_rest():
        load(gain_hbm, gain_v, 2).start()
        load(w1_hbm.at[0], w1, 3).start()
        for b in range(2):
            for f in range(4):
                load(r_hbm.at[0, pl.ds(64 * b, 64), pl.ds(256 * f, 256)], r_stage.at[b, f], 4).start()
        load(w2_hbm.at[0], w2.at[pl.ds(0, 96)], 5).start()

    barrier = pltpu.get_barrier_semaphore()

    def greet(device):
        pl.semaphore_signal(barrier, inc=1, device_id=device, device_id_type=MESH)

    for offset in FAR:
        greet({"section": section(offset)})
    greet({"tp": part ^ 5})
    load_streams()
    for offset in MIDDLE:
        greet({"section": section(offset)})
    for n in AROUND[1:]:
        greet({"tp": part ^ n})
    for offset in CLOSE + NEXT:
        greet({"section": section(offset)})
    load_rest()

    class Exchange:
        def __init__(self, peers, here, device, block, landing, bulk, n):
            self.peers, self.here, self.bulk = peers, here, bulk
            self.ss, self.rs = sems.at[2 * n], sems.at[2 * n + 1]

            def copy(to):
                return pltpu.make_async_remote_copy(
                    src_ref=block(to), dst_ref=landing(here), send_sem=self.ss, recv_sem=self.rs,
                    device_id=device(to), device_id_type=MESH,
                )

            self.copy = copy

        def send(self, peers=None):
            for to in peers or self.peers:
                self.copy(to).start()

        def receive(self):
            landed(self.bulk, self.rs)

        def drain(self):
            landed(self.bulk, self.ss)

    by_section = lambda to: {"section": to}
    by_part = lambda to: {"tp": to}
    by_place = lambda to: {"section": plane * PLACES + to}
    by_plane = lambda to: {"section": to * PLACES + place}
    far, middle, close, beside = ([section(offset) for offset in group] for group in (FAR, MIDDLE, CLOSE, NEXT))
    sections = far + middle + close + beside
    parts = [part ^ n for n in AROUND]
    places = [place ^ n for n in range(1, PLACES)]
    planes = [(plane + n) & 7 for n in (4, 3, 5, 2, 6, 1, 7)]
    xg = Exchange(sections, me, by_section, lambda p: sent.at[p], lambda p: held.at[p], held.at[pl.ds(0, 31)], 0)
    wx = Exchange(sections, me, by_section, lambda p: w_sent.at[p], lambda p: w_held.at[p], w_held.at[pl.ds(0, 31)], 1)
    ox = Exchange(sections, me, by_section, lambda p: o_sent.at[p], lambda p: o_held.at[p], o_held.at[pl.ds(0, 31)], 2)
    zx = Exchange(parts, part, by_part, lambda p: z_sent.at[p], lambda p: z_held.at[p], z_held.at[pl.ds(0, 7)], 3)
    ax = Exchange(parts, part, by_part, lambda p: act.at[part], lambda p: act.at[p], act.at[pl.ds(0, 7)], 4)
    dx = Exchange(parts, part, by_part, lambda p: d_sent.at[p], lambda p: d_held.at[p], d_held.at[pl.ds(0, 7)], 5)
    rx = Exchange(places, place, by_place, lambda p: r_sent.at[:, p], lambda p: r_held.at[p], r_held.at[pl.ds(0, 3)], 6)
    cx = Exchange(places, place, by_place, lambda p: c_sent.at[p], lambda p: c_held.at[:, p], c_sent.at[pl.ds(0, 3)], 7)
    sx = Exchange(planes, plane, by_plane, lambda p: s_sent.at[p], lambda p: s_held.at[p], s_held.at[pl.ds(0, 7)], 8)

    row, col = grid(256, 256)
    regroup = pick(((row >> 2) & 3) * 64 + (row >> 4) * 4 + (row & 3) == col)

    for b in range(2):
        landed(stage.at[b], in_sem.at[b])
        grouped = dot(regroup, stage[b].reshape(256, WIDTH)).astype(BF16)
        sent[pl.ds(16 * b, 16)] = grouped.reshape(16, 16, WIDTH)
    load(gain_hbm, gain_v, 2).wait()
    load(w1_hbm.at[0], w1, 3).wait()
    gain = gain_v[...].astype(F32)
    x = jnp.concatenate([stage[0, 3], stage[1, 3]], axis=0).astype(F32)
    product = dot(jnp.concatenate(halves(x * gain), axis=0), w1[...])
    squares = jnp.broadcast_to(jnp.sum(x * x, axis=1, keepdims=True), (TOKENS, 128))
    z_sent[...] = jnp.concatenate([product[:TOKENS] + product[TOKENS:], squares], axis=1).reshape(SHARDS, 16, 512)

    pl.semaphore_wait(barrier, SECTIONS - 1 + SHARDS - 1)
    zx.send()
    z_held[pl.ds(part, 1)] = z_sent[pl.ds(part, 1)]
    xg.send(middle + far)
    held[pl.ds(me, 1)] = sent[pl.ds(me, 1)]

    landed(r_stage, in_sem.at[4])
    load(w2_hbm.at[0], w2.at[pl.ds(0, 96)], 5).wait()
    for b in range(2):
        grouped = dot(regroup, r_stage[b].reshape(256, 256)).astype(BF16)
        r_sent[pl.ds(4 * b, 4)] = grouped.reshape(4, PLACES, 16, 256)
    rx.send()
    r_held[pl.ds(place, 1)] = r_sent[:, pl.ds(place, 1)].reshape(1, PLANES, 16, 256)

    zx.receive()
    total = z_held[0]
    for p in range(1, SHARDS):
        total = total + z_held[p]
    scale = lax.rsqrt(total[:, HIDDEN:] / FULL_WIDTH + 1e-05)
    own = jnp.concatenate([total[:, :HIDDEN] * scale[:, :1], scale], axis=1)
    act[pl.ds(part, 1)] = own.reshape(1, 16, 512)
    ax.send()
    xg.send(close + beside)

    rx.receive()
    running = jnp.zeros((PLANES, 16, 256), F32)
    for p in reversed(range(PLACES)):
        running = running + r_held[p].astype(F32)
        c_sent[p] = running.astype(BF16)
    s_sent[...] = running.astype(BF16)
    c_held[:, pl.ds(place, 1)] = c_sent[pl.ds(place, 1)].reshape(PLANES, 1, 16, 256)
    s_held[pl.ds(plane, 1)] = s_sent[pl.ds(plane, 1)]
    cx.send()

    w2[pl.ds(96, 32)] = jnp.zeros((32, HIDDEN), BF16)
    ax.receive()
    pre = act[:, :, :HIDDEN].reshape(TOKENS, HIDDEN)
    inverse = act[:, :, HIDDEN:].reshape(TOKENS, 128)[:, :1]
    square = pre * pre
    bend = jnp.tanh(C0 * pre * (1.0 + C1 * square))
    hidden = 0.5 * pre * (1.0 + bend)
    slope = 0.5 * (1.0 + bend) + 0.5 * pre * (1.0 - bend * bend) * (C0 * (1.0 + 3.0 * C1 * square))
    h_high, h_low = halves(hidden)
    mixing = dot_nt(h_high, w2[...]) + dot_nt(h_low, w2[...])
    row, col = grid(TOKENS, 128)
    mixing = jnp.where((col & 31) <= me, mixing, 0.0)
    w_sent[...] = mixing.reshape(SECTIONS, 4, 128)
    w_held[pl.ds(me, 1)] = w_sent[pl.ds(me, 1)]
    wx.send()
    sx.send()

    row, col = grid(128, 512)
    sel_m[...] = pick((row >> 2) * 16 + 12 + (row & 3) == col)
    fold_m[...] = pick((((row >> 2) & 3) * SHARDS + (row >> 4) == (col >> 4)) & ((row & 3) == (col & 3)))
    wide_m[...] = pick(((row >> 5) == (col >> 7)) & ((row & 31) == ((col >> 2) & 31)))
    row, col = grid(512, 128)
    same = (row & 3) == (col & 3)
    spread_m[...] = pick(((row >> 4) == (col >> 2)) & same)
    same_m[...] = jnp.where(same, 1.0, 0.0)
    which = (row >> 2) & 3
    kept_m[...] = jnp.where((which == (col >> 5)) & (which < 3) & ((col & 31) <= (row >> 4)), 1.0, 0.0)
    row, col = grid(128, 128)
    across_m[...] = pick((row >> 2) == (col & 31))
    row, col = grid(256, 256)
    ungroup_m[...] = pick(((col >> 2) & 3) * 64 + (col >> 4) * 4 + (col & 3) == row)
    for b in range(2):
        x = stage[b, 3].astype(F32)
        normed = (x * inverse[64 * b : 64 * b + 64] * gain).astype(BF16)
        normed_t[:, pl.ds(64 * b, 64)] = normed.T

    xg.receive()
    table = held[...].reshape(512, WIDTH)
    streams = dot(sel_m[...], table).astype(BF16)
    gram = dot_nt(table, streams)
    high, low = halves(gram * same_m[...])
    wide = (dot(high, across_m[...]) + dot(low, across_m[...])) * kept_m[...]
    high, low = halves(wide)
    d_sent[...] = (dot(fold_m[...], high) + dot(fold_m[...], low)).reshape(SHARDS, 16, 128)
    dx.send()
    d_held[pl.ds(part, 1)] = d_sent[pl.ds(part, 1)]

    wx.receive()
    mixing = w_held[...].reshape(128, 128).astype(BF16)
    mixing = dot(spread_m[...], dot(mixing, wide_m[...]).astype(BF16))
    row, col = grid(512, 128)
    which = (row >> 2) & 3
    weights = jnp.where(which == 0, mixing[:, :128], jnp.where(which == 1, mixing[:, 128:256], mixing[:, 256:384]))
    weights = jnp.where(which < 3, weights * same_m[...], 0.0)
    weights = weights.astype(BF16).T
    partial = [dot(weights, table[:, 256 * f : 256 * f + 256]) for f in range(4)]
    sx.receive()
    running = jnp.zeros((16, 256), F32)
    carried = [None] * PLANES
    for p in reversed(range(PLANES)):
        carried[p] = jnp.concatenate([running] * PLACES, axis=0)
        running = running + s_held[p].astype(F32)
    for b in range(2):
        stacked = jnp.concatenate([p[64 * b : 64 * b + 64] for p in partial], axis=0)
        block = dot(regroup, stacked.astype(BF16)) + jnp.concatenate(carried[4 * b : 4 * b + 4], axis=0)
        o_sent[pl.ds(16 * b, 16)] = block.astype(BF16).reshape(16, 16, 256)
    o_held[pl.ds(me, 1)] = o_sent[pl.ds(me, 1)]

    ox.send(middle + far)
    dx.receive()
    total = d_held[0]
    for p in range(1, SHARDS):
        total = total + d_held[p]
    for a in range(4):
        e_sent[a] = total[4 * a : 4 * a + 4]

    home, turn = me & 7, me >> 3

    def e_copy(a, b):
        return pltpu.make_async_remote_copy(
            src_ref=e_sent.at[a], dst_ref=e_held.at[me], send_sem=sems.at[18], recv_sem=sems.at[19],
            device_id={"section": SHARDS * a + part, "tp": b}, device_id_type=MESH,
        )

    def e_each(do):
        for a in range(4):
            for n in AROUND:
                do(e_copy(a, part ^ n))

            @pl.when((home != part) | (turn != a))
            def _(a=a):
                do(e_copy(a, part))

    def e_landed(sem):
        @pl.when(home == part)
        def _():
            landed(e_held.at[pl.ds(0, 31)], sem)

        @pl.when(home != part)
        def _():
            landed(e_held, sem)

    e_each(lambda copy: copy.start())
    ox.send(beside + close)

    @pl.when(home == part)
    def _():
        e_held[pl.ds(me, 1)] = e_sent[pl.ds(turn, 1)]

    cx.receive()
    near = [dot(ungroup_m[...], c_held[pl.ds(4 * b, 4)].reshape(256, 256)) for b in range(2)]
    for exchange in (zx, ax, rx, cx, sx, xg, wx, dx):
        exchange.drain()

    e_landed(sems.at[19])

    mix_grad = e_held[...].reshape(TOKENS, 128)
    g_high, g_low = halves(mix_grad)
    pre_grad = ((dot(g_high, w2[...]) + dot(g_low, w2[...])) * slope).astype(BF16)
    first_v[0] = dot(normed_t[...], pre_grad)
    second = dot_tn(g_high, h_high) + dot_tn(g_low, h_high) + dot_tn(g_high, h_low)
    second_v[0] = second[:96]
    along = jnp.sum(pre_grad.astype(F32) * pre, axis=1, keepdims=True)
    inner = inverse * inverse * along / FULL_WIDTH
    local = inverse * (dot_nt(pre_grad, w1[...]) * gain)

    e_landed(sems.at[18])
    ox.drain()
    ox.receive()
    for b in range(2):
        rows = slice(64 * b, 64 * b + 64)
        arrived = dot(ungroup_m[...], o_held[pl.ds(16 * b, 16)].reshape(256, 256)) + near[b]
        x = stage[b, 3].astype(F32)
        for f in range(4):
            lanes = slice(256 * f, 256 * f + 256)
            value = arrived[64 * f : 64 * f + 64] + (local[rows, lanes] - x[:, lanes] * inner[rows])
            out_v[0, pl.ds(64 * b, 64), pl.ds(256 * f, 256)] = value.astype(BF16)


def handover(out_in, first_in, second_in, out, first, second, sems):
    pairs = ((first_in, first), (out_in, out), (second_in, second))
    copies = [pltpu.make_async_copy(src, dst, sems.at[n]) for n, (src, dst) in enumerate(pairs)]
    for copy in copies:
        copy.start()
    for copy in copies:
        copy.wait()


def local(layer_outputs, stream_grads, residual_grads, norm_gain, first_weight, second_weight):
    hbm = pl.BlockSpec(memory_space=pltpu.HBM)
    vmem = pl.BlockSpec(memory_space=pltpu.VMEM)
    dma = pltpu.SemaphoreType.DMA
    by_section = lambda rows, lanes, dtype: pltpu.VMEM((SECTIONS, rows, lanes), dtype)
    by_part = lambda rows, lanes: pltpu.VMEM((SHARDS, rows, lanes), F32)
    by_place = lambda *lead: pltpu.VMEM((*lead, 16, 256), BF16)
    shapes = (
        jax.ShapeDtypeStruct((1, TOKENS, WIDTH), BF16),
        jax.ShapeDtypeStruct((1, WIDTH, HIDDEN), F32),
        jax.ShapeDtypeStruct((1, 96, HIDDEN), F32),
    )
    args = (layer_outputs, stream_grads, residual_grads, norm_gain, first_weight, jnp.swapaxes(second_weight, 1, 2))
    grads = pl.pallas_call(
        kernel,
        out_shape=shapes,
        in_specs=[hbm] * 6,
        out_specs=(vmem, vmem, vmem),
        scratch_shapes=[
            pltpu.VMEM((2, 4, 64, WIDTH), BF16),
            pltpu.VMEM((2, 4, 64, 256), BF16),
            pltpu.VMEM((1, WIDTH), BF16),
            pltpu.VMEM((WIDTH, HIDDEN), BF16),
            pltpu.VMEM((128, HIDDEN), BF16),
            pltpu.VMEM((512, 128), BF16),
            pltpu.VMEM((128, 512), BF16),
            pltpu.VMEM((128, 512), BF16),
            pltpu.VMEM((128, 128), BF16),
            pltpu.VMEM((128, 512), BF16),
            pltpu.VMEM((512, 128), F32),
            pltpu.VMEM((512, 128), F32),
            pltpu.VMEM((256, 256), BF16),
            pltpu.VMEM((WIDTH, TOKENS), BF16),
            by_section(16, WIDTH, BF16), by_section(16, WIDTH, BF16),
            by_place(PLANES, PLACES), by_place(PLACES, PLANES),
            by_place(PLACES, PLANES), by_place(PLANES, PLACES),
            by_place(PLANES), by_place(PLANES),
            by_section(4, 128, F32), by_section(4, 128, F32),
            by_section(16, 256, BF16), by_section(16, 256, BF16),
            by_part(16, 512), by_part(16, 512), by_part(16, 512),
            by_part(16, 128), by_part(16, 128),
            pltpu.VMEM((4, 4, 128), F32),
            by_section(4, 128, F32),
            dma((6,)), dma((20,)),
        ],
        compiler_params=pltpu.CompilerParams(
            collective_id=0, has_side_effects=True, vmem_limit_bytes=32 * 1024 * 1024
        ),
    )(*[pltpu.with_memory_space_constraint(a, pltpu.HBM) for a in args])
    grads = pl.pallas_call(
        handover,
        out_shape=shapes,
        in_specs=[vmem] * 3,
        out_specs=(hbm,) * 3,
        scratch_shapes=[dma((3,))],
        compiler_params=pltpu.CompilerParams(vmem_limit_bytes=8 * 1024 * 1024),
    )(*[pltpu.with_memory_space_constraint(g, pltpu.VMEM) for g in grads])
    return grads[0], grads[1], jnp.swapaxes(grads[2], 1, 2)


def solution(mesh):
    placed = (
        P("section", None, "tp"),
        P("section", None, None, "tp"),
        P("section", None, "tp"),
        P("section", "tp"),
        P("section", "tp", None),
        P("section", None, None),
    )
    return jax.shard_map(
        local,
        mesh=mesh,
        in_specs=placed,
        out_specs=(P("section", None, "tp"), P("section", "tp", None), P("section", None, None)),
        check_vma=False,
    )
```
